128 devices in a mesh: dp: 8 (over x, core), strand: 2 (over z_hi), ctx: 8 (over z_lo, y).
Axes of the slice: x: 4, y: 4, z: 4 (z_hi: 2, z_lo: 2; z = z_hi * 2 + z_lo), core: 2. Of those that a mesh axis runs over, the one named last changes fastest.
Arguments:
- qkv: bfloat16 [8, 2, 1024, 3, 2048], P('dp', 'strand', 'ctx'), may hold values from -8 to 8
- out_weight: bfloat16 [2048, 4096], P('ctx'), may hold values from -4 to 4
- cotangent: bfloat16 [8, 2, 1024, 4096], P('dp', 'strand', 'ctx'), may hold values from -1.796875 to 1.796875
Outputs:
- mixed: bfloat16 [8, 2, 1024, 4096], P('dp', 'strand', 'ctx')
- qkv_grad: bfloat16 [8, 2, 1024, 3, 2048], P('dp', 'strand', 'ctx')
- weight_grad: float32 [2048, 4096], P('ctx', ('dp', 'strand'))
The draws below stay inside these ranges and needn't reach their ends.
All inputs are finite; a program needn't handle non-finite values.
Results may differ from the reference program's by a relative error of at most 0.019.
Values may be sent and summed in bfloat16 or wider, within the bound.
No kernel may reach another device: no remote copies, remote signals or barrier semaphores. Data moves between devices by JAX's collectives and lax.ppermute only.
A program may use at most 192 MiB of HBM per device.

```python
import math
import jax
import jax.numpy as jnp
from jax import lax

D = 4096
HEADS = 16
DH = 128
SEQ = 1024
BATCH = 8
N_CTX = 8


def draw_qkv(key, part):
    key = jax.random.fold_in(key, 11)
    dims_all = (BATCH, 2, SEQ, 3, HEADS * DH)
    key_base = jax.random.fold_in(key, 0)
    result = jnp.clip(jax.random.normal(key_base, dims_all, jnp.float32), -6.0, 6.0)
    return result.astype(jnp.bfloat16)


def block_levels(stream_key, shape, shards, least, high):
    def one(dim, shards_of):
        draws = jax.random.uniform(jax.random.fold_in(jax.random.fold_in(stream_key, 6), dim), (shards_of,), jnp.float32, least / len(shards), high / len(shards))
        return jnp.repeat(jnp.exp(draws), shape[dim] // shards_of).reshape((-1,) + (1,) * (len(shape) - dim - 1))

    loudness = one(*shards[0])
    for cut in shards[1:]:
        loudness = loudness * one(*cut)
    return loudness


def noise(stream_key, shape, spread, most, cuts=(), held_as=jnp.bfloat16):
    values = jax.random.normal(stream_key, shape, jnp.float32) * spread
    if len(cuts) > 0:
        values = block_levels(stream_key, shape, cuts, -0.22, 0.18) * values
    return jnp.clip(values, min=-most, max=most).astype(held_as)


def setup_inputs(seed: int = 0) -> dict:
    keys = jax.random.split(jax.random.key(seed), 4)
    qkv = draw_qkv(jax.random.fold_in(keys[3], 71), 0)
    out_weight = noise(keys[1], (HEADS * DH, D), (max(HEADS * DH // SEQ, 1)) ** -0.5, 4.0, ((0, 8),))
    cotangent = noise(keys[2], (BATCH, 2, SEQ, D), 0.3, 1.796875, ((0, 8), (1, 2), (2, 8)))
    return dict(qkv=qkv, out_weight=out_weight, cotangent=cotangent)


def strand_forward(rows):
    scale = 1.0 / math.sqrt(DH)
    queries = rows[:, 0].reshape(SEQ, HEADS, DH)
    keys_all = rows[:, 1].reshape(SEQ, HEADS, DH)
    values_all = rows[:, 2].reshape(SEQ, HEADS, DH)
    scores = jnp.einsum('qhd,khd->hqk', queries.astype(jnp.float32), keys_all.astype(jnp.float32)) * scale
    peak = lax.optimization_barrier(jnp.max(scores, axis=-1, keepdims=True))
    expo = jnp.exp(scores - peak)
    probs32 = expo / lax.optimization_barrier(jnp.sum(expo, axis=-1, keepdims=True))
    probs = probs32.astype(jnp.bfloat16)
    attended = jnp.einsum('hqk,khd->qhd', probs.astype(jnp.float32), values_all.astype(jnp.float32))
    attended = attended.astype(jnp.bfloat16).reshape(SEQ, HEADS * DH)
    return (queries, keys_all, values_all, probs32, probs, attended)

def strand_backward(saved, upstream, out_weight):
    scale = 1.0 / math.sqrt(DH)
    queries, keys_all, values_all, probs32, probs, attended = saved
    weight_part = jnp.dot(attended.T, upstream, preferred_element_type=jnp.float32)
    grad_att = jnp.dot(upstream, out_weight.T, preferred_element_type=jnp.float32).astype(jnp.bfloat16)
    grad_att = grad_att.reshape(SEQ, HEADS, DH).astype(jnp.float32)
    grad_probs = jnp.einsum('qhd,khd->hqk', grad_att, values_all.astype(jnp.float32))
    grad_values = jnp.einsum('hqk,qhd->khd', probs.astype(jnp.float32), grad_att).astype(jnp.bfloat16)
    centre = lax.optimization_barrier(jnp.sum(grad_probs * probs32, axis=-1, keepdims=True))
    grad_scores = (probs32 * (grad_probs - centre) * scale).astype(jnp.bfloat16).astype(jnp.float32)
    grad_queries = jnp.einsum('hqk,khd->qhd', grad_scores, keys_all.astype(jnp.float32)).astype(jnp.bfloat16)
    grad_keys = jnp.einsum('hqk,qhd->khd', grad_scores, queries.astype(jnp.float32)).astype(jnp.bfloat16)
    stacked = jnp.stack([grad_queries, grad_keys, grad_values], axis=1).reshape(SEQ, 3, HEADS * DH)
    return (stacked, weight_part)

def reference(qkv, out_weight, cotangent):
    group_width = HEADS * DH // N_CTX
    weight_groups = out_weight.reshape(N_CTX, group_width, D).astype(jnp.float32)

    def project(attended):
        pieces = jnp.einsum('lgc,gcd->gld', attended.reshape(SEQ, N_CTX, group_width).astype(jnp.float32), weight_groups)
        pieces = lax.optimization_barrier(pieces.astype(jnp.bfloat16)).astype(jnp.float32)
        return lax.optimization_barrier(jnp.sum(pieces, axis=0))

    def one_pair(weight_total, inputs):
        pair_qkv, pair_cot = inputs
        first = strand_forward(pair_qkv[0])
        second = strand_forward(pair_qkv[1])
        proj_first = project(first[5])
        proj_second = project(second[5])
        mixed_pair = jnp.stack([proj_first + proj_second[::-1], proj_second + proj_first[::-1]]).astype(jnp.bfloat16)
        up_first = (pair_cot[0].astype(jnp.float32) + pair_cot[1][::-1].astype(jnp.float32)).astype(jnp.bfloat16)
        up_second = (pair_cot[1].astype(jnp.float32) + pair_cot[0][::-1].astype(jnp.float32)).astype(jnp.bfloat16)
        grads_first, weight_first = strand_backward(first, up_first, out_weight)
        grads_second, weight_second = strand_backward(second, up_second, out_weight)
        weight_total = weight_total + weight_first + weight_second
        return (weight_total, (mixed_pair, jnp.stack([grads_first, grads_second])))
    start_total = jnp.zeros((HEADS * DH, D), jnp.float32)
    total, (mixed, grads) = lax.scan(one_pair, start_total, (qkv, cotangent))
    return (mixed, grads, total)
```

```python
import functools
import math

import jax
import jax.numpy as jnp
from jax import lax
from jax.experimental import pallas as pl
from jax.experimental.pallas import tpu as pltpu
from jax.sharding import PartitionSpec as P

DH = 128
N = 8
SEQ = 1024
ROWS = SEQ // N
HALF = ROWS // 2
GW = 256
D = 4096
F32 = jnp.float32
BF16 = jnp.bfloat16
VMEM_LIMIT = 56 * 1024 * 1024


def flip_matrix(n):
    a = lax.broadcasted_iota(jnp.int32, (n, n), 0)
    b = lax.broadcasted_iota(jnp.int32, (n, n), 1)
    return (a + b == n - 1).astype(BF16)


def dot(a, b, ca, cb):
    return lax.dot_general(a, b, (((ca,), (cb,)), ((), ())), preferred_element_type=F32)


def params(**kw):
    return pltpu.CompilerParams(vmem_limit_bytes=VMEM_LIMIT, **kw)


def cost(flops, nbytes, trans=0):
    return pl.CostEstimate(flops=int(flops), bytes_accessed=int(nbytes), transcendentals=int(trans))


def struct(*shape, dtype=BF16):
    return jax.ShapeDtypeStruct(shape, dtype)


def split_kernel(c_ref, x_ref, *outs):
    for k in range(N):
        g = jnp.bitwise_xor(c_ref[0], k)
        outs[k][...] = x_ref[:, :, pl.ds(pl.multiple_of(g * GW, GW), GW)]


def split(c, x):
    return pl.pallas_call(
        split_kernel,
        in_specs=[pl.BlockSpec(memory_space=pltpu.SMEM), pl.BlockSpec(memory_space=pltpu.VMEM)],
        out_specs=[pl.BlockSpec(memory_space=pltpu.VMEM)] * N,
        out_shape=[struct(3, ROWS, GW)] * N,
        compiler_params=params(),
        cost_estimate=cost(0, 2 * 3 * ROWS * 2048 * 2),
        name="split",
    )(c, x)


def assemble_kernel(c_ref, *refs):
    out = refs[N]
    for k in range(N):
        g = jnp.bitwise_xor(c_ref[0], k)
        out[:, :, pl.ds(pl.multiple_of(g * GW, GW), GW)] = refs[k][...]


def assemble(c, blocks):
    return pl.pallas_call(
        assemble_kernel,
        in_specs=[pl.BlockSpec(memory_space=pltpu.SMEM)] + [pl.BlockSpec(memory_space=pltpu.VMEM)] * N,
        out_specs=pl.BlockSpec(memory_space=pltpu.VMEM),
        out_shape=struct(3, ROWS, 2048),
        compiler_params=params(),
        cost_estimate=cost(0, 2 * 3 * ROWS * 2048 * 2),
        name="assemble",
    )(c, *blocks)


def fwd_kernel(*refs):
    blocks = refs[:N]
    cat, att_own, att_send, probs_t = refs[N:]
    q = pl.program_id(1)

    @pl.when(q == 0)
    def _():
        flip = flip_matrix(HALF)
        for j in range(N):
            cat[1, ROWS * j : ROWS * (j + 1), :] = blocks[j][1]
            cat[2, ROWS * j : ROWS * (j + 1), :] = blocks[j][2]
            cat[0, HALF * j : HALF * (j + 1), :] = blocks[j][0, :HALF, :]
            mirrored = dot(flip, blocks[N - 1 - j][0, HALF:, :], 1, 0).astype(BF16)
            cat[0, 512 + HALF * j : 512 + HALF * (j + 1), :] = mirrored

    queries = cat[0, pl.ds(pl.multiple_of(q * 256, 256), 256), :]
    scores = dot(cat[1], queries, 1, 1) * (1.0 / math.sqrt(DH))
    peak = jnp.max(scores, axis=0, keepdims=True)
    expo = jnp.exp(scores - peak)
    probs = (expo * (1.0 / jnp.sum(expo, axis=0, keepdims=True))).astype(BF16)
    probs_t[0] = probs
    att = jnp.transpose(dot(cat[2], probs, 0, 0)).astype(BF16)

    @pl.when(q < 2)
    def _():
        att_own[...] = att

    @pl.when(q >= 2)
    def _():
        att_send[...] = att


def low_half(h, q):
    return (jnp.minimum(q, 1), h)


def high_half(h, q):
    return (jnp.maximum(q - 2, 0), h)


def attention_fwd(blocks):
    return pl.pallas_call(
        fwd_kernel,
        grid=(2, 4),
        in_specs=[pl.BlockSpec((3, ROWS, DH), lambda h, q: (0, 0, h))] * N,
        out_specs=[
            pl.BlockSpec((3, SEQ, DH), lambda h, q: (0, 0, h)),
            pl.BlockSpec((256, DH), low_half),
            pl.BlockSpec((256, DH), high_half),
            pl.BlockSpec((1, SEQ, 256), lambda h, q: (h, 0, q)),
        ],
        out_shape=[struct(3, SEQ, GW), struct(512, GW), struct(512, GW), struct(2, SEQ, SEQ)],
        compiler_params=params(dimension_semantics=("arbitrary", "arbitrary")),
        cost_estimate=cost(4 * 4 * SEQ * SEQ * DH, 10 << 20, 2 * SEQ * SEQ),
        name="attention_fwd",
    )(*blocks)


def bwd_kernel(cat, probs_t, g_own, g_recv, *refs):
    outs = refs[:N]
    dq, dk, dv = refs[N:]
    q = pl.program_id(1)
    queries = cat[0, pl.ds(pl.multiple_of(q * 256, 256), 256), :]
    grad = jnp.where(q < 2, g_own[...], g_recv[...])
    probs_low = probs_t[0]
    grad_probs = dot(cat[2], grad, 1, 1)
    probs = probs_low.astype(F32)
    product = probs * grad_probs
    centre = jnp.sum(product, axis=0, keepdims=True)
    grad_scores = ((product - probs * centre) * (1.0 / math.sqrt(DH))).astype(BF16)
    part_v = dot(probs_low, grad, 1, 0)
    part_k = dot(grad_scores, queries, 1, 0)

    @pl.when(q == 0)
    def _():
        dv[...] = part_v
        dk[...] = part_k

    @pl.when(q > 0)
    def _():
        dv[...] += part_v
        dk[...] += part_k

    part_q = jnp.transpose(dot(cat[1], grad_scores, 0, 0)).astype(BF16)
    dq[pl.ds(pl.multiple_of(q * 256, 256), 256), :] = part_q

    @pl.when(q == 3)
    def _():
        flip = flip_matrix(HALF)
        for j in range(N):
            outs[j][0, :HALF, :] = dq[HALF * j : HALF * (j + 1), :]
            low = 512 + HALF * (N - 1 - j)
            outs[j][0, HALF:, :] = dot(flip, dq[low : low + HALF, :], 1, 0).astype(BF16)
            outs[j][1] = dk[ROWS * j : ROWS * (j + 1), :].astype(BF16)
            outs[j][2] = dv[ROWS * j : ROWS * (j + 1), :].astype(BF16)


def attention_bwd(cat, probs_t, g_own, g_recv):
    return pl.pallas_call(
        bwd_kernel,
        grid=(2, 4),
        in_specs=[
            pl.BlockSpec((3, SEQ, DH), lambda h, q: (0, 0, h)),
            pl.BlockSpec((1, SEQ, 256), lambda h, q: (h, 0, q)),
            pl.BlockSpec((256, DH), low_half),
            pl.BlockSpec((256, DH), high_half),
        ],
        out_specs=[pl.BlockSpec((3, ROWS, DH), lambda h, q: (0, 0, h))] * N,
        out_shape=[struct(3, ROWS, GW)] * N,
        scratch_shapes=[pltpu.VMEM((SEQ, DH), BF16), pltpu.VMEM((SEQ, DH), F32), pltpu.VMEM((SEQ, DH), F32)],
        compiler_params=params(dimension_semantics=("arbitrary", "arbitrary")),
        cost_estimate=cost(8 * 2 * SEQ * SEQ * DH, 8 << 20),
        name="attention_bwd",
    )(cat, probs_t, g_own, g_recv)


def grad_kernel(*refs):
    pieces = refs[:9]
    w, out, acc = refs[9:]
    k = pl.program_id(0)
    rows = jnp.concatenate([p[...] for p in pieces], axis=0)
    part = dot(rows, w[...], 1, 1)

    @pl.when(k == 0)
    def _():
        acc[...] = part

    @pl.when(k > 0)
    def _():
        acc[...] += part

    @pl.when(k == 3)
    def _():
        out[...] = acc[...].astype(BF16)


def grad_attended(pieces, w):
    return pl.pallas_call(
        grad_kernel,
        grid=(4,),
        in_specs=[pl.BlockSpec((p.shape[0], 1024), lambda k: (0, k)) for p in pieces]
        + [pl.BlockSpec((GW, 1024), lambda k: (0, k))],
        out_specs=pl.BlockSpec((512, GW), lambda k: (0, 0)),
        out_shape=struct(512, GW),
        scratch_shapes=[pltpu.VMEM((512, GW), F32)],
        compiler_params=params(),
        cost_estimate=cost(2 * 512 * GW * D, 7 << 20),
        name="grad_attended",
    )(*pieces, w)


def project_kernel(own, recv, w, *outs):
    both = (own[...].astype(F32) + recv[...].astype(F32)).astype(BF16)
    part = dot(both, w[...], 1, 0).astype(BF16)
    low = 0
    for out in outs:
        out[...] = part[low : low + out.shape[0], :]
        low += out.shape[0]


def project(own, recv, w):
    rows = (64, 64, 32, 32, 64, 64, 64, 64, 64)
    return pl.pallas_call(
        project_kernel,
        grid=(4,),
        in_specs=[
            pl.BlockSpec((512, GW), lambda k: (0, 0)),
            pl.BlockSpec((512, GW), lambda k: (0, 0)),
            pl.BlockSpec((GW, 1024), lambda k: (0, k)),
        ],
        out_specs=[pl.BlockSpec((r, 1024), lambda k: (0, k)) for r in rows],
        out_shape=[struct(r, D) for r in rows],
        compiler_params=params(),
        cost_estimate=cost(2 * 512 * GW * D, 7 << 20),
        name="project",
    )(own, recv, w)


def weight_kernel(d_ref, own, recv, *refs):
    pieces = refs[:9]
    out_own, out_other = refs[9:]
    both = (own[...].astype(F32) + recv[...].astype(F32)).astype(BF16)
    rows = jnp.concatenate([p[...] for p in pieces], axis=0)
    part = dot(both, rows, 0, 0).astype(BF16)
    first, second = part[:, :512], part[:, 512:]
    core = jnp.bitwise_and(d_ref[0], 1)
    out_own[0] = jnp.where(core == 0, first, second)
    out_other[0] = jnp.where(core == 0, second, first)


def weight_part(d, own, recv, pieces):
    def columns(x, d_ref):
        return (0, jnp.bitwise_xor(lax.shift_right_logical(d_ref[0], 1), x))

    return pl.pallas_call(
        weight_kernel,
        grid_spec=pltpu.PrefetchScalarGridSpec(
            num_scalar_prefetch=1,
            grid=(4,),
            in_specs=[pl.BlockSpec((512, GW), lambda x, d_ref: (0, 0))] * 2
            + [pl.BlockSpec((p.shape[0], 1024), columns) for p in pieces],
            out_specs=[pl.BlockSpec((1, GW, 512), lambda x, d_ref: (x, 0, 0))] * 2,
        ),
        out_shape=[struct(4, GW, 512)] * 2,
        compiler_params=params(),
        cost_estimate=cost(2 * 512 * GW * D, 7 << 20),
        name="weight_part",
    )(d, own, recv, *pieces)


def by_xor(x, axis, k):
    return lax.ppermute(x, axis, [(i, i ^ k) for i in range(N)])


def mirror(x):
    return lax.ppermute(x, ("strand", "ctx"), [(i, 2 * N - 1 - i) for i in range(2 * N)])


def other_strand(x):
    return lax.ppermute(x, "strand", [(0, 1), (1, 0)])


def flip_rows(x):
    return dot(flip_matrix(x.shape[0]), x, 1, 0)


def add(*terms):
    total = terms[0].astype(F32)
    for t in terms[1:]:
        total = total + t.astype(F32)
    return total


def gather_rows(u):
    y1, y3, z = (by_xor(u, "ctx", k) for k in (1, 3, 4))
    y2a = by_xor(y3[:32], "ctx", 1)
    y2b = by_xor(y1[32:], "ctx", 3)
    zy1 = by_xor(z, "ctx", 1)
    zy3 = by_xor(z, "ctx", 3)
    zy2 = by_xor(jnp.concatenate([y2a, y2b], axis=0), "ctx", 4)
    return [u, y1, y2a, y2b, y3, z, zy1, zy2, zy3]


def scatter_rows(parts):
    p0, p1, p2a, p2b, p3, p4, p5, p6, p7 = parts
    r5 = by_xor(p5, "ctx", 1)
    r7 = by_xor(p7, "ctx", 3)
    r6 = by_xor(p6, "ctx", 4)
    p2a = add(p2a, r6[:32]).astype(BF16)
    p2b = add(p2b, r6[32:]).astype(BF16)
    p4 = add(p4, r5, r7).astype(BF16)
    r2a = by_xor(p2a, "ctx", 1)
    r2b = by_xor(p2b, "ctx", 3)
    r4 = by_xor(p4, "ctx", 4)
    p3 = add(p3, jnp.pad(r2a, ((0, 32), (0, 0)))).astype(BF16)
    p1 = add(p1, jnp.pad(r2b, ((32, 0), (0, 0)))).astype(BF16)
    r3 = by_xor(p3, "ctx", 3)
    r1 = by_xor(p1, "ctx", 1)
    return add(p0, r1, r3, r4)


def body(qkv, out_weight, cotangent):
    c = lax.axis_index("ctx").astype(jnp.int32).reshape(1)
    d = lax.axis_index("dp").astype(jnp.int32).reshape(1)
    s = lax.axis_index("strand")
    mine = jnp.transpose(qkv[0, 0], (1, 0, 2))
    cot = cotangent[0, 0]

    cot_recv = mirror(cot[HALF:])
    sent = split(c, mine)
    blocks = [sent[0]] + [by_xor(sent[k], "ctx", k) for k in range(1, N)]

    upstream = (cot[:HALF].astype(F32) + flip_rows(cot_recv)).astype(BF16)
    pieces = gather_rows(upstream)

    cat, att_own, att_send, probs_t = attention_fwd(blocks)
    att_recv = other_strand(att_send)
    partial = project(att_own, att_recv, out_weight)

    g_own = grad_attended(pieces, out_weight)
    g_recv = other_strand(g_own)

    mixed_own = scatter_rows(partial).astype(BF16)
    mixed_recv = mirror(mixed_own)
    mixed = jnp.concatenate([mixed_own, flip_rows(mixed_recv).astype(BF16)], axis=0)

    grads = attention_bwd(cat, probs_t, g_own, g_recv)
    back = [grads[0]] + [by_xor(grads[k], "ctx", k) for k in range(1, N)]
    qkv_grad = jnp.transpose(assemble(c, back), (1, 0, 2))

    w_own, w_other = weight_part(d, att_own, att_recv, pieces)
    w_sum = add(w_own, by_xor(w_other, "dp", 1)).astype(BF16)
    w_chip = add(w_sum[0], *[by_xor(w_sum[x], "dp", 2 * x) for x in range(1, 4)])
    first, second = w_chip[:, :GW], w_chip[:, GW:]
    w_keep = jnp.where(s == 0, first, second)
    w_send = jnp.where(s == 0, second, first).astype(BF16)
    weight_grad = w_keep + other_strand(w_send).astype(F32)
    return (mixed[None, None], qkv_grad[None, None], weight_grad)


def solution(mesh):
    placed = (P("dp", "strand", "ctx", None, None), P("ctx", None), P("dp", "strand", "ctx", None))
    return jax.shard_map(
        body,
        mesh=mesh,
        in_specs=placed,
        out_specs=(
            P("dp", "strand", "ctx", None),
            P("dp", "strand", "ctx", None, None),
            P("ctx", ("dp", "strand")),
        ),
        check_vma=False,
    )
```

```python
import functools
import math

import jax
import jax.numpy as jnp
from jax import lax
from jax.experimental import pallas as pl
from jax.experimental.pallas import tpu as pltpu
from jax.sharding import PartitionSpec as P

DH = 128
N = 8
SEQ = 1024
ROWS = SEQ // N
HALF = ROWS // 2
GW = 256
D = 4096
F32 = jnp.float32
BF16 = jnp.bfloat16
VMEM_LIMIT = 56 * 1024 * 1024


def flip_matrix(n):
    a = lax.broadcasted_iota(jnp.int32, (n, n), 0)
    b = lax.broadcasted_iota(jnp.int32, (n, n), 1)
    return (a + b == n - 1).astype(BF16)


def dot(a, b, ca, cb):
    return lax.dot_general(a, b, (((ca,), (cb,)), ((), ())), preferred_element_type=F32)


def params(**kw):
    return pltpu.CompilerParams(vmem_limit_bytes=VMEM_LIMIT, **kw)


def cost(flops, nbytes, trans=0):
    return pl.CostEstimate(flops=int(flops), bytes_accessed=int(nbytes), transcendentals=int(trans))


def struct(*shape, dtype=BF16):
    return jax.ShapeDtypeStruct(shape, dtype)


ANY = pl.BlockSpec(memory_space=pl.ANY)


def split_kernel(x_ref, out):
    for g in range(N):
        out[g] = x_ref[:, :, GW * g : GW * (g + 1)]


def split(x):
    return pl.pallas_call(
        split_kernel,
        in_specs=[pl.BlockSpec(memory_space=pltpu.VMEM)],
        out_specs=pl.BlockSpec(memory_space=pltpu.VMEM),
        out_shape=struct(N, 3, ROWS, GW),
        compiler_params=params(),
        cost_estimate=cost(0, 2 * 3 * ROWS * 2048 * 2),
        name="split",
    )(x)


def assemble_kernel(blocks, out):
    for g in range(N):
        out[:, :, GW * g : GW * (g + 1)] = blocks[g]


def assemble(blocks):
    return pl.pallas_call(
        assemble_kernel,
        in_specs=[pl.BlockSpec(memory_space=pltpu.VMEM)],
        out_specs=pl.BlockSpec(memory_space=pltpu.VMEM),
        out_shape=struct(3, ROWS, 2048),
        compiler_params=params(),
        cost_estimate=cost(0, 2 * 3 * ROWS * 2048 * 2),
        name="assemble",
    )(blocks)


def upstream_kernel(cot, recv, after, out):
    flipped = dot(flip_matrix(HALF), recv[...], 1, 0)
    out[...] = (cot[...].astype(F32) + flipped).astype(BF16)


def upstream_rows(cot, recv, after):
    return pl.pallas_call(
        upstream_kernel,
        grid=(2,),
        in_specs=[pl.BlockSpec((HALF, 2048), lambda k: (0, k))] * 2 + [ANY],
        out_specs=pl.BlockSpec((HALF, 2048), lambda k: (0, k)),
        out_shape=struct(HALF, D),
        compiler_params=params(),
        cost_estimate=cost(2 * 64 * 64 * D, 3 << 19),
        name="upstream_rows",
    )(cot, recv, after)


def fwd_kernel(c_ref, *refs):
    blocks = refs[:N]
    after, cat, att_own, att_send, probs_t = refs[N:]
    q = pl.program_id(0)

    @pl.when(q == 0)
    def _():
        flip = flip_matrix(HALF)
        for j in range(N):
            cat[1, ROWS * j : ROWS * (j + 1), :] = blocks[j][0, 1]
            cat[2, ROWS * j : ROWS * (j + 1), :] = blocks[j][0, 2]
            cat[0, HALF * j : HALF * (j + 1), :] = blocks[j][0, 0, :HALF, :]
            mirrored = dot(flip, blocks[N - 1 - j][0, 0, HALF:, :], 1, 0).astype(BF16)
            cat[0, 512 + HALF * j : 512 + HALF * (j + 1), :] = mirrored

    for h in range(2):
        cols = slice(DH * h, DH * (h + 1))
        queries = cat[0, pl.ds(pl.multiple_of(q * 256, 256), 256), cols]
        scores = dot(cat[1, :, cols], queries, 1, 1) * (1.0 / math.sqrt(DH))
        peak = jnp.max(scores, axis=0, keepdims=True)
        expo = jnp.exp(scores - peak)
        probs = (expo * (1.0 / jnp.sum(expo, axis=0, keepdims=True))).astype(BF16)
        probs_t[h] = probs
        att = jnp.transpose(dot(cat[2, :, cols], probs, 0, 0)).astype(BF16)

        @pl.when(q < 2)
        def _():
            att_own[:, cols] = att

        @pl.when(q >= 2)
        def _():
            att_send[:, cols] = att


def low_half(q, *_):
    return (jnp.minimum(q, 1), 0)


def high_half(q, *_):
    return (jnp.maximum(q - 2, 0), 0)


def attention_fwd(c, blocks, after):
    def block(j):
        return pl.BlockSpec((1, 3, ROWS, GW), lambda q, c_ref: (jnp.bitwise_xor(c_ref[0], j), 0, 0, 0))

    return pl.pallas_call(
        fwd_kernel,
        grid_spec=pltpu.PrefetchScalarGridSpec(
            num_scalar_prefetch=1,
            grid=(4,),
            in_specs=[block(j) for j in range(N)] + [ANY],
            out_specs=[
                pl.BlockSpec((3, SEQ, GW), lambda q, c_ref: (0, 0, 0)),
                pl.BlockSpec((256, GW), low_half),
                pl.BlockSpec((256, GW), high_half),
                pl.BlockSpec((2, SEQ, 256), lambda q, c_ref: (0, 0, q)),
            ],
        ),
        out_shape=[struct(3, SEQ, GW), struct(512, GW), struct(512, GW), struct(2, SEQ, SEQ)],
        compiler_params=params(),
        cost_estimate=cost(4 * 4 * SEQ * SEQ * DH, 10 << 20, 2 * SEQ * SEQ),
        name="attention_fwd",
    )(c, *([blocks] * N), after)


def bwd_kernel(c_ref, cat, probs_t, g_own, g_recv, after, after2, out, dq, dk, dv):
    q = pl.program_id(0)
    rows = pl.ds(pl.multiple_of(q * 256, 256), 256)
    for h in range(2):
        cols = slice(DH * h, DH * (h + 1))
        queries = cat[0, rows, cols]
        grad = jnp.where(q < 2, g_own[:, cols], g_recv[:, cols])
        probs_low = probs_t[h]
        grad_probs = dot(cat[2, :, cols], grad, 1, 1)
        probs = probs_low.astype(F32)
        product = probs * grad_probs
        centre = jnp.sum(product, axis=0, keepdims=True)
        grad_scores = ((product - probs * centre) * (1.0 / math.sqrt(DH))).astype(BF16)
        part_v = dot(probs_low, grad, 1, 0)
        part_k = dot(grad_scores, queries, 1, 0)

        @pl.when(q == 0)
        def _():
            dv[:, cols] = part_v
            dk[:, cols] = part_k

        @pl.when(q > 0)
        def _():
            dv[:, cols] += part_v
            dk[:, cols] += part_k

        dq[rows, cols] = jnp.transpose(dot(cat[1, :, cols], grad_scores, 0, 0)).astype(BF16)

    @pl.when(q == 3)
    def _():
        flip = flip_matrix(HALF)
        for j in range(N):
            to = jnp.bitwise_xor(c_ref[0], j)
            low = 512 + HALF * (N - 1 - j)
            out[to, 0, :HALF, :] = dq[HALF * j : HALF * (j + 1), :]
            out[to, 0, HALF:, :] = dot(flip, dq[low : low + HALF, :], 1, 0).astype(BF16)
            out[to, 1] = dk[ROWS * j : ROWS * (j + 1), :].astype(BF16)
            out[to, 2] = dv[ROWS * j : ROWS * (j + 1), :].astype(BF16)


def attention_bwd(c, cat, probs_t, g_own, g_recv, after, after2):
    return pl.pallas_call(
        bwd_kernel,
        grid_spec=pltpu.PrefetchScalarGridSpec(
            num_scalar_prefetch=1,
            grid=(4,),
            in_specs=[
                pl.BlockSpec((3, SEQ, GW), lambda q, c_ref: (0, 0, 0)),
                pl.BlockSpec((2, SEQ, 256), lambda q, c_ref: (0, 0, q)),
                pl.BlockSpec((256, GW), low_half),
                pl.BlockSpec((256, GW), high_half),
                ANY,
                ANY,
            ],
            out_specs=pl.BlockSpec((N, 3, ROWS, GW), lambda q, c_ref: (0, 0, 0, 0)),
            scratch_shapes=[pltpu.VMEM((SEQ, GW), BF16), pltpu.VMEM((SEQ, GW), F32), pltpu.VMEM((SEQ, GW), F32)],
        ),
        out_shape=struct(N, 3, ROWS, GW),
        compiler_params=params(),
        cost_estimate=cost(8 * 2 * SEQ * SEQ * DH, 8 << 20),
        name="attention_bwd",
    )(c, cat, probs_t, g_own, g_recv, after, after2)


def grad_kernel(*refs):
    pieces = refs[:9]
    w, after, out, acc = refs[9:]
    k = pl.program_id(0)
    rows = jnp.concatenate([p[...] for p in pieces], axis=0)
    part = dot(rows, w[...], 1, 1)

    @pl.when(k == 0)
    def _():
        acc[...] = part

    @pl.when(k > 0)
    def _():
        acc[...] += part

    @pl.when(k == 3)
    def _():
        out[...] = acc[...].astype(BF16)


def grad_attended(pieces, w, after):
    return pl.pallas_call(
        grad_kernel,
        grid=(4,),
        in_specs=[pl.BlockSpec((p.shape[0], 1024), lambda k: (0, k)) for p in pieces]
        + [pl.BlockSpec((GW, 1024), lambda k: (0, k)), ANY],
        out_specs=pl.BlockSpec((512, GW), lambda k: (0, 0)),
        out_shape=struct(512, GW),
        scratch_shapes=[pltpu.VMEM((512, GW), F32)],
        compiler_params=params(),
        cost_estimate=cost(2 * 512 * GW * D, 7 << 20),
        name="grad_attended",
    )(*pieces, w, after)


def project_kernel(own, recv, w, *outs):
    both = (own[...].astype(F32) + recv[...].astype(F32)).astype(BF16)
    part = dot(both, w[...], 1, 0).astype(BF16)
    low = 0
    for out in outs:
        out[...] = part[low : low + out.shape[0], :]
        low += out.shape[0]


def project(own, recv, w):
    rows = (64, 64, 32, 32, 64, 64, 64, 64, 64)
    return pl.pallas_call(
        project_kernel,
        grid=(4,),
        in_specs=[
            pl.BlockSpec((512, GW), lambda k: (0, 0)),
            pl.BlockSpec((512, GW), lambda k: (0, 0)),
            pl.BlockSpec((GW, 1024), lambda k: (0, k)),
        ],
        out_specs=[pl.BlockSpec((r, 1024), lambda k: (0, k)) for r in rows],
        out_shape=[struct(r, D) for r in rows],
        compiler_params=params(),
        cost_estimate=cost(2 * 512 * GW * D, 7 << 20),
        name="project",
    )(own, recv, w)


def weight_kernel(d_ref, own, recv, *refs):
    pieces = refs[:9]
    out_own, out_other = refs[10:]
    both = (own[...].astype(F32) + recv[...].astype(F32)).astype(BF16)
    rows = jnp.concatenate([p[...] for p in pieces], axis=0)
    part = dot(both, rows, 0, 0).astype(BF16)
    first, second = part[:, :512], part[:, 512:]
    core = jnp.bitwise_and(d_ref[0], 1)
    out_own[0] = jnp.where(core == 0, first, second)
    out_other[0] = jnp.where(core == 0, second, first)


def weight_part(d, own, recv, pieces, after):
    def columns(x, d_ref):
        return (0, jnp.bitwise_xor(lax.shift_right_logical(d_ref[0], 1), x))

    return pl.pallas_call(
        weight_kernel,
        grid_spec=pltpu.PrefetchScalarGridSpec(
            num_scalar_prefetch=1,
            grid=(4,),
            in_specs=[pl.BlockSpec((512, GW), lambda x, d_ref: (0, 0))] * 2
            + [pl.BlockSpec((p.shape[0], 1024), columns) for p in pieces]
            + [ANY],
            out_specs=[pl.BlockSpec((1, GW, 512), lambda x, d_ref: (x, 0, 0))] * 2,
        ),
        out_shape=[struct(4, GW, 512)] * 2,
        compiler_params=params(),
        cost_estimate=cost(2 * 512 * GW * D, 7 << 20),
        name="weight_part",
    )(d, own, recv, *pieces, after)


def by_xor(x, axis, k):
    return lax.ppermute(x, axis, [(i, i ^ k) for i in range(N)])


def mirror(x):
    return lax.ppermute(x, ("strand", "ctx"), [(i, 2 * N - 1 - i) for i in range(2 * N)])


def other_strand(x):
    return lax.ppermute(x, "strand", [(0, 1), (1, 0)])


def flip_rows(x):
    return dot(flip_matrix(x.shape[0]), x, 1, 0)


def add(*terms):
    total = terms[0].astype(F32)
    for t in terms[1:]:
        total = total + t.astype(F32)
    return total


def relay_kernel(y1, y3, after, low, high):
    low[...] = y3[:32, :]
    high[...] = y1[32:, :]


def relay(y1, y3, after):
    return pl.pallas_call(
        relay_kernel,
        in_specs=[pl.BlockSpec(memory_space=pltpu.VMEM)] * 2 + [ANY],
        out_specs=[pl.BlockSpec(memory_space=pltpu.VMEM)] * 2,
        out_shape=[struct(32, D)] * 2,
        compiler_params=params(),
        cost_estimate=cost(0, 3 << 19),
        name="relay",
    )(y1, y3, after)


def gather_rows(u, after):
    y1, y3, z = (by_xor(u, "ctx", k) for k in (1, 3, 4))
    low, high = relay(y1, y3, after)
    y2a = by_xor(low, "ctx", 1)
    y2b = by_xor(high, "ctx", 3)
    zy1 = by_xor(z, "ctx", 1)
    zy3 = by_xor(z, "ctx", 3)
    zy2 = by_xor(jnp.concatenate([y2a, y2b], axis=0), "ctx", 4)
    return [u, y1, y2a, y2b, y3, z, zy1, zy2, zy3]


def scatter_rows(parts):
    p0, p1, p2a, p2b, p3, p4, p5, p6, p7 = parts
    r5 = by_xor(p5, "ctx", 1)
    r7 = by_xor(p7, "ctx", 3)
    r6 = by_xor(p6, "ctx", 4)
    p2a = add(p2a, r6[:32]).astype(BF16)
    p2b = add(p2b, r6[32:]).astype(BF16)
    p4 = add(p4, r5, r7).astype(BF16)
    r2a = by_xor(p2a, "ctx", 1)
    r2b = by_xor(p2b, "ctx", 3)
    r4 = by_xor(p4, "ctx", 4)
    p3 = add(p3, jnp.pad(r2a, ((0, 32), (0, 0)))).astype(BF16)
    p1 = add(p1, jnp.pad(r2b, ((32, 0), (0, 0)))).astype(BF16)
    r3 = by_xor(p3, "ctx", 3)
    r1 = by_xor(p1, "ctx", 1)
    return add(p0, r1, r3, r4), p4


def body(qkv, out_weight, cotangent):
    c = lax.axis_index("ctx").astype(jnp.int32).reshape(1)
    d = lax.axis_index("dp").astype(jnp.int32).reshape(1)
    s = lax.axis_index("strand")
    mine = jnp.transpose(qkv[0, 0], (1, 0, 2))
    cot = cotangent[0, 0]

    cot_recv = mirror(cot[HALF:])
    blocks = lax.all_to_all(split(mine), "ctx", split_axis=0, concat_axis=0, tiled=True)

    upstream = upstream_rows(cot, cot_recv, blocks)
    cat, att_own, att_send, probs_t = attention_fwd(c, blocks, upstream)
    att_recv = other_strand(att_send)
    pieces = gather_rows(upstream, att_own)

    partial = project(att_own, att_recv, out_weight)
    mixed_rows, relayed = scatter_rows(partial)
    mixed_own = mixed_rows.astype(BF16)
    mixed_recv = mirror(mixed_own)
    mixed = jnp.concatenate([mixed_own, flip_rows(mixed_recv).astype(BF16)], axis=0)

    g_own = grad_attended(pieces, out_weight, partial[0])
    g_recv = other_strand(g_own)
    w_own, w_other = weight_part(d, att_own, att_recv, pieces, g_own)

    grads = attention_bwd(c, cat, probs_t, g_own, g_recv, w_own, relayed)
    back = lax.all_to_all(grads, "ctx", split_axis=0, concat_axis=0, tiled=True)
    qkv_grad = jnp.transpose(assemble(back), (1, 0, 2))

    w_sum = add(w_own, by_xor(w_other, "dp", 1)).astype(BF16)
    w_chip = add(w_sum[0], *[by_xor(w_sum[x], "dp", 2 * x) for x in range(1, 4)])
    first, second = w_chip[:, :GW], w_chip[:, GW:]
    w_keep = jnp.where(s == 0, first, second)
    w_send = jnp.where(s == 0, second, first).astype(BF16)
    weight_grad = w_keep + other_strand(w_send).astype(F32)
    return (mixed[None, None], qkv_grad[None, None], weight_grad)


def solution(mesh):
    placed = (P("dp", "strand", "ctx", None, None), P("ctx", None), P("dp", "strand", "ctx", None))
    return jax.shard_map(
        body,
        mesh=mesh,
        in_specs=placed,
        out_specs=(
            P("dp", "strand", "ctx", None),
            P("dp", "strand", "ctx", None, None),
            P("ctx", ("dp", "strand")),
        ),
        check_vma=False,
    )
```

```python
import functools
import math

import jax
import jax.numpy as jnp
from jax import lax
from jax.experimental import pallas as pl
from jax.experimental.pallas import tpu as pltpu
from jax.sharding import PartitionSpec as P

DH = 128
N = 8
SEQ = 1024
ROWS = SEQ // N
HALF = ROWS // 2
GW = 256
D = 4096
F32 = jnp.float32
BF16 = jnp.bfloat16
VMEM_LIMIT = 56 * 1024 * 1024


def flip_matrix(n):
    a = lax.broadcasted_iota(jnp.int32, (n, n), 0)
    b = lax.broadcasted_iota(jnp.int32, (n, n), 1)
    return (a + b == n - 1).astype(BF16)


def dot(a, b, ca, cb):
    return lax.dot_general(a, b, (((ca,), (cb,)), ((), ())), preferred_element_type=F32)


def params(**kw):
    return pltpu.CompilerParams(vmem_limit_bytes=VMEM_LIMIT, **kw)


def cost(flops, nbytes, trans=0):
    return pl.CostEstimate(flops=int(flops), bytes_accessed=int(nbytes), transcendentals=int(trans))


def struct(*shape, dtype=BF16):
    return jax.ShapeDtypeStruct(shape, dtype)


ANY = pl.BlockSpec(memory_space=pl.ANY)


def gate_kernel(*refs):
    pass


def gate(xs, after):
    return pl.pallas_call(
        gate_kernel,
        in_specs=[ANY] * (len(xs) + len(after)),
        out_specs=[ANY] * len(xs),
        out_shape=[struct(*x.shape) for x in xs],
        input_output_aliases={i: i for i in range(len(xs))},
        compiler_params=params(),
        cost_estimate=cost(0, 0),
        name="gate",
    )(*xs, *after)


def gate_kernel(*refs):
    pass


def gate(xs, after):
    return pl.pallas_call(
        gate_kernel,
        in_specs=[ANY] * (len(xs) + len(after)),
        out_specs=[ANY] * len(xs),
        out_shape=[struct(*x.shape) for x in xs],
        input_output_aliases={i: i for i in range(len(xs))},
        compiler_params=params(),
        cost_estimate=cost(0, 0),
        name="gate",
    )(*xs, *after)


def split_kernel(x_ref, out):
    for g in range(N):
        out[g] = x_ref[:, :, GW * g : GW * (g + 1)]


def split(x):
    return pl.pallas_call(
        split_kernel,
        in_specs=[pl.BlockSpec(memory_space=pltpu.VMEM)],
        out_specs=pl.BlockSpec(memory_space=pltpu.VMEM),
        out_shape=struct(N, 3, ROWS, GW),
        compiler_params=params(),
        cost_estimate=cost(0, 2 * 3 * ROWS * 2048 * 2),
        name="split",
    )(x)


def assemble_kernel(blocks, out):
    for g in range(N):
        out[:, :, GW * g : GW * (g + 1)] = blocks[g]


def assemble(blocks):
    return pl.pallas_call(
        assemble_kernel,
        in_specs=[pl.BlockSpec(memory_space=pltpu.VMEM)],
        out_specs=pl.BlockSpec(memory_space=pltpu.VMEM),
        out_shape=struct(3, ROWS, 2048),
        compiler_params=params(),
        cost_estimate=cost(0, 2 * 3 * ROWS * 2048 * 2),
        name="assemble",
    )(blocks)


def upstream_kernel(cot, recv, out):
    flipped = dot(flip_matrix(HALF), recv[...], 1, 0)
    out[...] = (cot[...].astype(F32) + flipped).astype(BF16)


def upstream_rows(cot, recv):
    return pl.pallas_call(
        upstream_kernel,
        grid=(2,),
        in_specs=[pl.BlockSpec((HALF, 2048), lambda k: (0, k))] * 2,
        out_specs=pl.BlockSpec((HALF, 2048), lambda k: (0, k)),
        out_shape=struct(HALF, D),
        compiler_params=params(),
        cost_estimate=cost(2 * 64 * 64 * D, 2 << 20),
        name="upstream_rows",
    )(cot, recv)


def fwd_kernel(c_ref, blocks, *refs):
    cat, att_own, att_send, probs_t = refs[-4:]
    q = pl.program_id(0)

    @pl.when(q == 0)
    def _():
        flip = flip_matrix(HALF)
        for j in range(N):
            of = jnp.bitwise_xor(c_ref[0], j)
            far = jnp.bitwise_xor(c_ref[0], N - 1 - j)
            cat[1, ROWS * j : ROWS * (j + 1), :] = blocks[of, 1]
            cat[2, ROWS * j : ROWS * (j + 1), :] = blocks[of, 2]
            cat[0, HALF * j : HALF * (j + 1), :] = blocks[of, 0, :HALF, :]
            mirrored = dot(flip, blocks[far, 0, HALF:, :], 1, 0).astype(BF16)
            cat[0, 512 + HALF * j : 512 + HALF * (j + 1), :] = mirrored

    for h in range(2):
        cols = slice(DH * h, DH * (h + 1))
        queries = cat[0, pl.ds(pl.multiple_of(q * 256, 256), 256), cols]
        scores = dot(cat[1, :, cols], queries, 1, 1) * (1.0 / math.sqrt(DH))
        peak = jnp.max(scores, axis=0, keepdims=True)
        expo = jnp.exp(scores - peak)
        probs = (expo * (1.0 / jnp.sum(expo, axis=0, keepdims=True))).astype(BF16)
        probs_t[h] = probs
        att = jnp.transpose(dot(cat[2, :, cols], probs, 0, 0)).astype(BF16)

        @pl.when(q < 2)
        def _():
            att_own[:, cols] = att

        @pl.when(q >= 2)
        def _():
            att_send[:, cols] = att


def low_half(q, *_):
    return (jnp.minimum(q, 1), 0)


def high_half(q, *_):
    return (jnp.maximum(q - 2, 0), 0)


def attention_fwd(c, blocks, after):
    return pl.pallas_call(
        fwd_kernel,
        grid_spec=pltpu.PrefetchScalarGridSpec(
            num_scalar_prefetch=1,
            grid=(4,),
            in_specs=[pl.BlockSpec((N, 3, ROWS, GW), lambda q, c_ref: (0, 0, 0, 0))] + [ANY] * len(after),
            out_specs=[
                pl.BlockSpec((3, SEQ, GW), lambda q, c_ref: (0, 0, 0)),
                pl.BlockSpec((256, GW), low_half),
                pl.BlockSpec((256, GW), high_half),
                pl.BlockSpec((2, SEQ, 256), lambda q, c_ref: (0, 0, q)),
            ],
        ),
        out_shape=[struct(3, SEQ, GW), struct(512, GW), struct(512, GW), struct(2, SEQ, SEQ)],
        compiler_params=params(),
        cost_estimate=cost(4 * 4 * SEQ * SEQ * DH, 10 << 20, 2 * SEQ * SEQ),
        name="attention_fwd",
    )(c, blocks, *after)


def bwd_kernel(c_ref, cat, probs_t, g_own, g_recv, *refs):
    out, dq, dk, dv = refs[-4:]
    q = pl.program_id(0)
    rows = pl.ds(pl.multiple_of(q * 256, 256), 256)
    queries = cat[0, rows, :]
    grad = jnp.where(q < 2, g_own[...], g_recv[...])
    probs_low = probs_t[0]
    grad_probs = dot(cat[2], grad, 1, 1)
    probs = probs_low.astype(F32)
    product = probs * grad_probs
    centre = jnp.sum(product, axis=0, keepdims=True)
    grad_scores = ((product - probs * centre) * (1.0 / math.sqrt(DH))).astype(BF16)
    part_v = dot(probs_low, grad, 1, 0)
    part_k = dot(grad_scores, queries, 1, 0)

    @pl.when(q == 0)
    def _():
        dv[...] = part_v
        dk[...] = part_k

    @pl.when(q > 0)
    def _():
        dv[...] += part_v
        dk[...] += part_k

    dq[rows, :] = jnp.transpose(dot(cat[1], grad_scores, 0, 0)).astype(BF16)

    @pl.when(q == 3)
    def _():
        flip = flip_matrix(HALF)
        for j in range(N):
            to = jnp.bitwise_xor(c_ref[0], j)
            low = 512 + HALF * (N - 1 - j)
            out[to, 0, :HALF, :] = dq[HALF * j : HALF * (j + 1), :]
            out[to, 0, HALF:, :] = dot(flip, dq[low : low + HALF, :], 1, 0).astype(BF16)
            out[to, 1] = dk[ROWS * j : ROWS * (j + 1), :].astype(BF16)
            out[to, 2] = dv[ROWS * j : ROWS * (j + 1), :].astype(BF16)


def attention_bwd(c, h, cat, probs_t, g_own, g_recv, filled, after):
    return pl.pallas_call(
        bwd_kernel,
        grid_spec=pltpu.PrefetchScalarGridSpec(
            num_scalar_prefetch=1,
            grid=(4,),
            in_specs=[
                pl.BlockSpec((3, SEQ, DH), lambda q, c_ref: (0, 0, h)),
                pl.BlockSpec((1, SEQ, 256), lambda q, c_ref: (h, 0, q)),
                pl.BlockSpec((256, DH), lambda q, c_ref: (jnp.minimum(q, 1), h)),
                pl.BlockSpec((256, DH), lambda q, c_ref: (jnp.maximum(q - 2, 0), h)),
            ]
            + [ANY] * (len(filled) + len(after)),
            out_specs=pl.BlockSpec((N, 3, ROWS, DH), lambda q, c_ref: (0, 0, 0, h)),
            scratch_shapes=[pltpu.VMEM((SEQ, DH), BF16), pltpu.VMEM((SEQ, DH), F32), pltpu.VMEM((SEQ, DH), F32)],
        ),
        out_shape=struct(N, 3, ROWS, GW),
        input_output_aliases={5 + i: i for i in range(len(filled))},
        compiler_params=params(),
        cost_estimate=cost(4 * 2 * SEQ * SEQ * DH, 4 << 20),
        name="attention_bwd",
    )(c, cat, probs_t, g_own, g_recv, *filled, *after)


def grad_kernel(*refs):
    pieces = refs[:N]
    w = refs[N]
    out, acc = refs[-2:]
    k = pl.program_id(0)
    rows = jnp.concatenate([p[...] for p in pieces], axis=0)
    part = dot(rows, w[...], 1, 1)

    @pl.when(k == 0)
    def _():
        acc[...] = part

    @pl.when(k > 0)
    def _():
        acc[...] += part

    @pl.when(k == 3)
    def _():
        out[...] = acc[...].astype(BF16)


def grad_attended(pieces, w, after):
    return pl.pallas_call(
        grad_kernel,
        grid=(4,),
        in_specs=[pl.BlockSpec((p.shape[0], 1024), lambda k: (0, k)) for p in pieces]
        + [pl.BlockSpec((GW, 1024), lambda k: (0, k))]
        + [ANY] * len(after),
        out_specs=pl.BlockSpec((512, GW), lambda k: (0, 0)),
        out_shape=struct(512, GW),
        scratch_shapes=[pltpu.VMEM((512, GW), F32)],
        compiler_params=params(),
        cost_estimate=cost(2 * 512 * GW * D, 7 << 20),
        name="grad_attended",
    )(*pieces, w, *after)


def project_kernel(own, recv, w, *outs):
    both = (own[...].astype(F32) + recv[...].astype(F32)).astype(BF16)
    part = dot(both, w[...], 1, 0).astype(BF16)
    low = 0
    for out in outs:
        out[...] = part[low : low + out.shape[0], :]
        low += out.shape[0]


def project(own, recv, w):
    rows = (HALF,) * N
    return pl.pallas_call(
        project_kernel,
        grid=(4,),
        in_specs=[
            pl.BlockSpec((512, GW), lambda k: (0, 0)),
            pl.BlockSpec((512, GW), lambda k: (0, 0)),
            pl.BlockSpec((GW, 1024), lambda k: (0, k)),
        ],
        out_specs=[pl.BlockSpec((r, 1024), lambda k: (0, k)) for r in rows],
        out_shape=[struct(r, D) for r in rows],
        compiler_params=params(),
        cost_estimate=cost(2 * 512 * GW * D, 7 << 20),
        name="project",
    )(own, recv, w)


def weight_kernel(d_ref, own, recv, *refs):
    pieces = refs[:N]
    out_own, out_other = refs[-2:]
    both = (own[...].astype(F32) + recv[...].astype(F32)).astype(BF16)
    rows = jnp.concatenate([p[...] for p in pieces], axis=0)
    part = dot(both, rows, 0, 0).astype(BF16)
    first, second = part[:, :512], part[:, 512:]
    core = jnp.bitwise_and(d_ref[0], 1)
    out_own[0] = jnp.where(core == 0, first, second)
    out_other[0] = jnp.where(core == 0, second, first)


def weight_part(d, own, recv, pieces, after):
    def columns(x, d_ref):
        return (0, jnp.bitwise_xor(lax.shift_right_logical(d_ref[0], 1), x))

    return pl.pallas_call(
        weight_kernel,
        grid_spec=pltpu.PrefetchScalarGridSpec(
            num_scalar_prefetch=1,
            grid=(4,),
            in_specs=[pl.BlockSpec((512, GW), lambda x, d_ref: (0, 0))] * 2
            + [pl.BlockSpec((p.shape[0], 1024), columns) for p in pieces]
            + [ANY] * len(after),
            out_specs=[pl.BlockSpec((1, GW, 512), lambda x, d_ref: (x, 0, 0))] * 2,
        ),
        out_shape=[struct(4, GW, 512)] * 2,
        compiler_params=params(),
        cost_estimate=cost(2 * 512 * GW * D, 7 << 20),
        name="weight_part",
    )(d, own, recv, *pieces, *after)


def by_xor(x, axis, k):
    return lax.ppermute(x, axis, [(i, i ^ k) for i in range(N)])


def mirror(x):
    return lax.ppermute(x, ("strand", "ctx"), [(i, 2 * N - 1 - i) for i in range(2 * N)])


def other_strand(x):
    return lax.ppermute(x, "strand", [(0, 1), (1, 0)])


def flip_rows(x):
    return dot(flip_matrix(x.shape[0]), x, 1, 0)


def add(*terms):
    total = terms[0].astype(F32)
    for t in terms[1:]:
        total = total + t.astype(F32)
    return total


def mix_sum_kernel(p0, r1, r3, r4, out):
    out[...] = add(p0[...], r1[...], r3[...], r4[...]).astype(BF16)


def mix_sum(*terms):
    return pl.pallas_call(
        mix_sum_kernel,
        grid=(2,),
        in_specs=[pl.BlockSpec((HALF, 2048), lambda k: (0, k))] * 4,
        out_specs=pl.BlockSpec((HALF, 2048), lambda k: (0, k)),
        out_shape=struct(HALF, D),
        compiler_params=params(),
        cost_estimate=cost(0, 5 << 19),
        name="mix_sum",
    )(*terms)


def mix_out_kernel(own, recv, out):
    out[:HALF, :] = own[...]
    out[HALF:, :] = dot(flip_matrix(HALF), recv[...], 1, 0).astype(BF16)


def mix_out(own, recv):
    return pl.pallas_call(
        mix_out_kernel,
        grid=(2,),
        in_specs=[pl.BlockSpec((HALF, 2048), lambda k: (0, k))] * 2,
        out_specs=pl.BlockSpec((ROWS, 2048), lambda k: (0, k)),
        out_shape=struct(ROWS, D),
        compiler_params=params(),
        cost_estimate=cost(0, 2 << 20),
        name="mix_out",
    )(own, recv)


def body(qkv, out_weight, cotangent):
    c = lax.axis_index("ctx").astype(jnp.int32).reshape(1)
    d = lax.axis_index("dp").astype(jnp.int32).reshape(1)
    s = lax.axis_index("strand")
    mine = jnp.transpose(qkv[0, 0], (1, 0, 2))
    cot = cotangent[0, 0]

    cot_recv = mirror(cot[HALF:])
    (sent,) = gate([split(mine)], [cot_recv])
    blocks = lax.all_to_all(sent, "ctx", split_axis=0, concat_axis=0, tiled=True)

    u = upstream_rows(cot, cot_recv)
    y1, y3, z = by_xor(u, "ctx", 1), by_xor(u, "ctx", 3), by_xor(u, "ctx", 4)
    y2, zy1, zy3 = by_xor(y3, "ctx", 1), by_xor(z, "ctx", 1), by_xor(z, "ctx", 3)
    cat, att_own, att_send, probs_t = attention_fwd(c, blocks, [y1, y3, z])
    (att_send,) = gate([att_send], [y2, zy3])
    att_recv = other_strand(att_send)
    zy2 = by_xor(y2, "ctx", 4)
    pieces = [u, y1, y2, y3, z, zy1, zy2, zy3]

    p0, p1, p2, p3, p4, p5, p6, p7 = project(att_own, att_recv, out_weight)
    r5, r7, r6 = by_xor(p5, "ctx", 1), by_xor(p7, "ctx", 3), by_xor(p6, "ctx", 4)
    g_own = grad_attended(pieces, out_weight, [p0])
    g_recv = other_strand(g_own)
    p4 = add(p4, r5, r7).astype(BF16)
    p2 = add(p2, r6).astype(BF16)
    r4, r2 = by_xor(p4, "ctx", 4), by_xor(p2, "ctx", 1)
    w_own, w_other = weight_part(d, att_own, att_recv, pieces, [g_own, p4, p2])
    grads = attention_bwd(c, 0, cat, probs_t, g_own, g_recv, [], [w_own])
    p3 = add(p3, r2).astype(BF16)
    p3, p1 = gate([p3, p1], [grads])
    r3, r1 = by_xor(p3, "ctx", 3), by_xor(p1, "ctx", 1)
    grads = attention_bwd(c, 1, cat, probs_t, g_own, g_recv, [grads], [p3, p1])
    mixed_own = mix_sum(p0, r1, r3, r4)
    back = lax.all_to_all(grads, "ctx", split_axis=0, concat_axis=0, tiled=True)
    mixed = mix_out(mixed_own, mirror(mixed_own))
    qkv_grad = jnp.transpose(assemble(back), (1, 0, 2))

    w_sum = add(w_own, by_xor(w_other, "dp", 1)).astype(BF16)
    (w_sum,) = gate([w_sum], [mixed_own])
    w_chip = add(w_sum[0], *[by_xor(w_sum[x], "dp", 2 * x) for x in range(1, 4)])
    first, second = w_chip[:, :GW], w_chip[:, GW:]
    w_keep = jnp.where(s == 0, first, second)
    w_send = jnp.where(s == 0, second, first).astype(BF16)
    weight_grad = w_keep + other_strand(w_send).astype(F32)
    return (mixed[None, None], qkv_grad[None, None], weight_grad)


def solution(mesh):
    placed = (P("dp", "strand", "ctx", None, None), P("ctx", None), P("dp", "strand", "ctx", None))
    return jax.shard_map(
        body,
        mesh=mesh,
        in_specs=placed,
        out_specs=(
            P("dp", "strand", "ctx", None),
            P("dp", "strand", "ctx", None, None),
            P("ctx", ("dp", "strand")),
        ),
        check_vma=False,
    )
```

```python
import functools
import math

import jax
import jax.numpy as jnp
from jax import lax
from jax.experimental import pallas as pl
from jax.experimental.pallas import tpu as pltpu
from jax.sharding import PartitionSpec as P

DH = 128
N = 8
SEQ = 1024
ROWS = SEQ // N
HALF = ROWS // 2
GW = 256
D = 4096
F32 = jnp.float32
BF16 = jnp.bfloat16
VMEM_LIMIT = 36 * 1024 * 1024


def flip_matrix(n):
    a = lax.broadcasted_iota(jnp.int32, (n, n), 0)
    b = lax.broadcasted_iota(jnp.int32, (n, n), 1)
    return (a + b == n - 1).astype(BF16)


def dot(a, b, ca, cb):
    return lax.dot_general(a, b, (((ca,), (cb,)), ((), ())), preferred_element_type=F32)


def params(limit=VMEM_LIMIT):
    return pltpu.CompilerParams(vmem_limit_bytes=limit)


def cost(flops, nbytes, trans=0):
    return pl.CostEstimate(flops=int(flops), bytes_accessed=int(nbytes), transcendentals=int(trans))


def struct(*shape, dtype=BF16):
    return jax.ShapeDtypeStruct(shape, dtype)


ANY = pl.BlockSpec(memory_space=pl.ANY)


def gate_kernel(*refs):
    pass


def gate(xs, after):
    return pl.pallas_call(
        gate_kernel,
        in_specs=[ANY] * (len(xs) + len(after)),
        out_specs=[ANY] * len(xs),
        out_shape=[struct(*x.shape) for x in xs],
        input_output_aliases={i: i for i in range(len(xs))},
        compiler_params=params(),
        cost_estimate=cost(0, 0),
        name="gate",
    )(*xs, *after)


def gate_kernel(*refs):
    pass


def gate(xs, after):
    return pl.pallas_call(
        gate_kernel,
        in_specs=[ANY] * (len(xs) + len(after)),
        out_specs=[ANY] * len(xs),
        out_shape=[struct(*x.shape) for x in xs],
        input_output_aliases={i: i for i in range(len(xs))},
        compiler_params=params(),
        cost_estimate=cost(0, 0),
        name="gate",
    )(*xs, *after)


def split_kernel(x_ref, out):
    for g in range(N):
        out[g] = x_ref[:, :, GW * g : GW * (g + 1)]


def split(x):
    return pl.pallas_call(
        split_kernel,
        in_specs=[pl.BlockSpec(memory_space=pltpu.VMEM)],
        out_specs=pl.BlockSpec(memory_space=pltpu.VMEM),
        out_shape=struct(N, 3, ROWS, GW),
        compiler_params=params(),
        cost_estimate=cost(0, 2 * 3 * ROWS * 2048 * 2),
        name="split",
    )(x)


def assemble_kernel(first, second, out):
    for g in range(N):
        out[:, :, GW * g : GW * g + DH] = first[g]
        out[:, :, GW * g + DH : GW * (g + 1)] = second[g]


def assemble(first, second):
    return pl.pallas_call(
        assemble_kernel,
        in_specs=[pl.BlockSpec(memory_space=pltpu.VMEM)] * 2,
        out_specs=pl.BlockSpec(memory_space=pltpu.VMEM),
        out_shape=struct(3, ROWS, 2048),
        compiler_params=params(),
        cost_estimate=cost(0, 2 * 3 * ROWS * 2048 * 2),
        name="assemble",
    )(first, second)


def upstream_kernel(cot, recv, out):
    flipped = dot(flip_matrix(HALF), recv[...], 1, 0)
    out[...] = (cot[...].astype(F32) + flipped).astype(BF16)


def upstream_rows(cot, recv):
    return pl.pallas_call(
        upstream_kernel,
        grid=(2,),
        in_specs=[pl.BlockSpec((HALF, 2048), lambda k: (0, k))] * 2,
        out_specs=pl.BlockSpec((HALF, 2048), lambda k: (0, k)),
        out_shape=struct(HALF, D),
        compiler_params=params(),
        cost_estimate=cost(2 * 64 * 64 * D, 2 << 20),
        name="upstream_rows",
    )(cot, recv)


def fwd_kernel(c_ref, blocks, *refs):
    cat, att_own, att_send, probs_t = refs[-4:]
    q = pl.program_id(0)

    @pl.when(q == 0)
    def _():
        flip = flip_matrix(HALF)
        for j in range(N):
            of = jnp.bitwise_xor(c_ref[0], j)
            far = jnp.bitwise_xor(c_ref[0], N - 1 - j)
            cat[1, ROWS * j : ROWS * (j + 1), :] = blocks[of, 1]
            cat[2, ROWS * j : ROWS * (j + 1), :] = blocks[of, 2]
            cat[0, HALF * j : HALF * (j + 1), :] = blocks[of, 0, :HALF, :]
            mirrored = dot(flip, blocks[far, 0, HALF:, :], 1, 0).astype(BF16)
            cat[0, 512 + HALF * j : 512 + HALF * (j + 1), :] = mirrored

    for h in range(2):
        cols = slice(DH * h, DH * (h + 1))
        queries = cat[0, pl.ds(pl.multiple_of(q * 256, 256), 256), cols]
        scores = dot(cat[1, :, cols], queries, 1, 1) * (1.0 / math.sqrt(DH))
        peak = jnp.max(scores, axis=0, keepdims=True)
        expo = jnp.exp(scores - peak)
        probs = (expo * (1.0 / jnp.sum(expo, axis=0, keepdims=True))).astype(BF16)
        probs_t[h] = probs
        att = jnp.transpose(dot(cat[2, :, cols], probs, 0, 0)).astype(BF16)

        @pl.when(q < 2)
        def _():
            att_own[:, cols] = att

        @pl.when(q >= 2)
        def _():
            att_send[:, cols] = att


def low_half(q, *_):
    return (jnp.minimum(q, 1), 0)


def high_half(q, *_):
    return (jnp.maximum(q - 2, 0), 0)


def attention_fwd(c, blocks, after):
    return pl.pallas_call(
        fwd_kernel,
        grid_spec=pltpu.PrefetchScalarGridSpec(
            num_scalar_prefetch=1,
            grid=(4,),
            in_specs=[pl.BlockSpec((N, 3, ROWS, GW), lambda q, c_ref: (0, 0, 0, 0))] + [ANY] * len(after),
            out_specs=[
                pl.BlockSpec((3, SEQ, GW), lambda q, c_ref: (0, 0, 0)),
                pl.BlockSpec((256, GW), low_half),
                pl.BlockSpec((256, GW), high_half),
                pl.BlockSpec((2, SEQ, 256), lambda q, c_ref: (0, 0, q)),
            ],
        ),
        out_shape=[struct(3, SEQ, GW), struct(512, GW), struct(512, GW), struct(2, SEQ, SEQ)],
        compiler_params=params(63 * 1024 * 1024),
        cost_estimate=cost(4 * 4 * SEQ * SEQ * DH, 10 << 20, 2 * SEQ * SEQ),
        name="attention_fwd",
    )(c, blocks, *after)


def bwd_kernel(c_ref, cat, probs_t, g_own, g_recv, *refs):
    out, dq, dk, dv = refs[-4:]
    q = pl.program_id(0)
    rows = pl.ds(pl.multiple_of(q * 256, 256), 256)
    queries = cat[0, rows, :]
    grad = jnp.where(q < 2, g_own[...], g_recv[...])
    probs_low = probs_t[0]
    grad_probs = dot(cat[2], grad, 1, 1)
    probs = probs_low.astype(F32)
    product = probs * grad_probs
    centre = jnp.sum(product, axis=0, keepdims=True)
    grad_scores = ((product - probs * centre) * (1.0 / math.sqrt(DH))).astype(BF16)
    part_v = dot(probs_low, grad, 1, 0)
    part_k = dot(grad_scores, queries, 1, 0)

    @pl.when(q == 0)
    def _():
        dv[...] = part_v
        dk[...] = part_k

    @pl.when(q > 0)
    def _():
        dv[...] += part_v
        dk[...] += part_k

    dq[rows, :] = jnp.transpose(dot(cat[1], grad_scores, 0, 0)).astype(BF16)

    @pl.when(q == 3)
    def _():
        flip = flip_matrix(HALF)
        for j in range(N):
            to = jnp.bitwise_xor(c_ref[0], j)
            low = 512 + HALF * (N - 1 - j)
            out[to, 0, :HALF, :] = dq[HALF * j : HALF * (j + 1), :]
            out[to, 0, HALF:, :] = dot(flip, dq[low : low + HALF, :], 1, 0).astype(BF16)
            out[to, 1] = dk[ROWS * j : ROWS * (j + 1), :].astype(BF16)
            out[to, 2] = dv[ROWS * j : ROWS * (j + 1), :].astype(BF16)


def attention_bwd(c, h, cat, probs_t, g_own, g_recv, after):
    return pl.pallas_call(
        bwd_kernel,
        grid_spec=pltpu.PrefetchScalarGridSpec(
            num_scalar_prefetch=1,
            grid=(4,),
            in_specs=[
                pl.BlockSpec((3, SEQ, DH), lambda q, c_ref: (0, 0, h)),
                pl.BlockSpec((1, SEQ, 256), lambda q, c_ref: (h, 0, q)),
                pl.BlockSpec((256, DH), lambda q, c_ref: (jnp.minimum(q, 1), h)),
                pl.BlockSpec((256, DH), lambda q, c_ref: (jnp.maximum(q - 2, 0), h)),
            ]
            + [ANY] * len(after),
            out_specs=pl.BlockSpec((N, 3, ROWS, DH), lambda q, c_ref: (0, 0, 0, 0)),
            scratch_shapes=[pltpu.VMEM((SEQ, DH), BF16), pltpu.VMEM((SEQ, DH), F32), pltpu.VMEM((SEQ, DH), F32)],
        ),
        out_shape=struct(N, 3, ROWS, DH),
        compiler_params=params(),
        cost_estimate=cost(4 * 2 * SEQ * SEQ * DH, 4 << 20),
        name="attention_bwd",
    )(c, cat, probs_t, g_own, g_recv, *after)


def grad_kernel(*refs):
    pieces = refs[:N]
    w = refs[N]
    out, acc = refs[-2:]
    k = pl.program_id(0)
    rows = jnp.concatenate([p[...] for p in pieces], axis=0)
    part = dot(rows, w[...], 1, 1)

    @pl.when(k == 0)
    def _():
        acc[...] = part

    @pl.when(k > 0)
    def _():
        acc[...] += part

    @pl.when(k == 3)
    def _():
        out[...] = acc[...].astype(BF16)


def grad_attended(pieces, w, after):
    return pl.pallas_call(
        grad_kernel,
        grid=(4,),
        in_specs=[pl.BlockSpec((p.shape[0], 1024), lambda k: (0, k)) for p in pieces]
        + [pl.BlockSpec((GW, 1024), lambda k: (0, k))]
        + [ANY] * len(after),
        out_specs=pl.BlockSpec((512, GW), lambda k: (0, 0)),
        out_shape=struct(512, GW),
        scratch_shapes=[pltpu.VMEM((512, GW), F32)],
        compiler_params=params(),
        cost_estimate=cost(2 * 512 * GW * D, 7 << 20),
        name="grad_attended",
    )(*pieces, w, *after)


def project_kernel(own, recv, w, *outs):
    both = (own[...].astype(F32) + recv[...].astype(F32)).astype(BF16)
    part = dot(both, w[...], 1, 0).astype(BF16)
    low = 0
    for out in outs:
        out[...] = part[low : low + out.shape[0], :]
        low += out.shape[0]


def project(own, recv, w):
    rows = (HALF,) * N
    return pl.pallas_call(
        project_kernel,
        grid=(4,),
        in_specs=[
            pl.BlockSpec((512, GW), lambda k: (0, 0)),
            pl.BlockSpec((512, GW), lambda k: (0, 0)),
            pl.BlockSpec((GW, 1024), lambda k: (0, k)),
        ],
        out_specs=[pl.BlockSpec((r, 1024), lambda k: (0, k)) for r in rows],
        out_shape=[struct(r, D) for r in rows],
        compiler_params=params(63 * 1024 * 1024),
        cost_estimate=cost(2 * 512 * GW * D, 7 << 20),
        name="project",
    )(own, recv, w)


def weight_kernel(d_ref, own, recv, *refs):
    pieces = refs[:N]
    out_own, out_other = refs[-2:]
    both = (own[...].astype(F32) + recv[...].astype(F32)).astype(BF16)
    rows = jnp.concatenate([p[...] for p in pieces], axis=0)
    part = dot(both, rows, 0, 0).astype(BF16)
    first, second = part[:, :512], part[:, 512:]
    core = jnp.bitwise_and(d_ref[0], 1)
    out_own[0] = jnp.where(core == 0, first, second)
    out_other[0] = jnp.where(core == 0, second, first)


def weight_part(d, own, recv, pieces, after):
    def columns(x, d_ref):
        return (0, jnp.bitwise_xor(lax.shift_right_logical(d_ref[0], 1), x))

    return pl.pallas_call(
        weight_kernel,
        grid_spec=pltpu.PrefetchScalarGridSpec(
            num_scalar_prefetch=1,
            grid=(4,),
            in_specs=[pl.BlockSpec((512, GW), lambda x, d_ref: (0, 0))] * 2
            + [pl.BlockSpec((p.shape[0], 1024), columns) for p in pieces]
            + [ANY] * len(after),
            out_specs=[pl.BlockSpec((1, GW, 512), lambda x, d_ref: (x, 0, 0))] * 2,
        ),
        out_shape=[struct(4, GW, 512)] * 2,
        compiler_params=params(),
        cost_estimate=cost(2 * 512 * GW * D, 7 << 20),
        name="weight_part",
    )(d, own, recv, *pieces, *after)


def weight_sum_kernel(own, recv, *refs):
    for x in range(4):
        refs[x - 4][...] = add(own[x], recv[x]).astype(BF16)


def weight_sum(own, recv, after):
    return pl.pallas_call(
        weight_sum_kernel,
        in_specs=[pl.BlockSpec(memory_space=pltpu.VMEM)] * 2 + [ANY] * len(after),
        out_specs=[pl.BlockSpec(memory_space=pltpu.VMEM)] * 4,
        out_shape=[struct(GW, 512)] * 4,
        compiler_params=params(),
        cost_estimate=cost(0, 3 << 20),
        name="weight_sum",
    )(own, recv, *after)


def by_xor(x, axis, k):
    return lax.ppermute(x, axis, [(i, i ^ k) for i in range(N)])


def exchange(x):
    return lax.all_to_all(x, "ctx", split_axis=0, concat_axis=0, tiled=True)


def mirror(x):
    return lax.ppermute(x, ("strand", "ctx"), [(i, 2 * N - 1 - i) for i in range(2 * N)])


def other_strand(x):
    return lax.ppermute(x, "strand", [(0, 1), (1, 0)])


def flip_rows(x):
    return dot(flip_matrix(x.shape[0]), x, 1, 0)


def add(*terms):
    total = terms[0].astype(F32)
    for t in terms[1:]:
        total = total + t.astype(F32)
    return total


def mix_sum_kernel(p0, r1, r3, r4, *refs):
    out = refs[-1]
    out[...] = add(p0[...], r1[...], r3[...], r4[...]).astype(BF16)


def mix_sum(terms, after):
    return pl.pallas_call(
        mix_sum_kernel,
        grid=(2,),
        in_specs=[pl.BlockSpec((HALF, 2048), lambda k: (0, k))] * 4 + [ANY] * len(after),
        out_specs=pl.BlockSpec((HALF, 2048), lambda k: (0, k)),
        out_shape=struct(HALF, D),
        compiler_params=params(),
        cost_estimate=cost(0, 5 << 19),
        name="mix_sum",
    )(*terms, *after)


def mix_out_kernel(own, recv, out):
    out[:HALF, :] = own[...]
    out[HALF:, :] = dot(flip_matrix(HALF), recv[...], 1, 0).astype(BF16)


def mix_out(own, recv):
    return pl.pallas_call(
        mix_out_kernel,
        grid=(2,),
        in_specs=[pl.BlockSpec((HALF, 2048), lambda k: (0, k))] * 2,
        out_specs=pl.BlockSpec((ROWS, 2048), lambda k: (0, k)),
        out_shape=struct(ROWS, D),
        compiler_params=params(),
        cost_estimate=cost(0, 2 << 20),
        name="mix_out",
    )(own, recv)


def body(qkv, out_weight, cotangent):
    c = lax.axis_index("ctx").astype(jnp.int32).reshape(1)
    d = lax.axis_index("dp").astype(jnp.int32).reshape(1)
    s = lax.axis_index("strand")
    mine = jnp.transpose(qkv[0, 0], (1, 0, 2))
    cot = cotangent[0, 0]

    cot_recv = mirror(cot[HALF:])
    (sent,) = gate([split(mine)], [cot_recv])
    blocks = exchange(sent)

    u = upstream_rows(cot, cot_recv)
    y1, y3, z = by_xor(u, "ctx", 1), by_xor(u, "ctx", 3), by_xor(u, "ctx", 4)
    y2, zy1, zy3 = by_xor(y3, "ctx", 1), by_xor(y1, "ctx", 4), by_xor(z, "ctx", 3)
    cat, att_own, att_send, probs_t = attention_fwd(c, blocks, [y1, y3, z])
    att_send, zy3 = gate([att_send, zy3], [y2, zy1])
    att_recv = other_strand(att_send)
    zy2 = by_xor(zy3, "ctx", 1)
    pieces = [u, y1, y2, y3, z, zy1, zy2, zy3]

    p0, p1, p2, p3, p4, p5, p6, p7 = project(att_own, att_recv, out_weight)
    r6, r7, r2 = by_xor(p6, "ctx", 3), by_xor(p7, "ctx", 4), by_xor(p2, "ctx", 1)
    g_own = grad_attended(pieces, out_weight, [p0])
    g_recv = other_strand(g_own)
    p5 = add(p5, r6).astype(BF16)
    r5 = by_xor(p5, "ctx", 4)
    w_own, w_other = weight_part(d, att_own, att_recv, pieces, [g_own, p5])
    p3 = add(p3, r7, r2).astype(BF16)
    r3 = by_xor(p3, "ctx", 3)
    grads0 = attention_bwd(c, 0, cat, probs_t, g_own, g_recv, [w_own, p3])
    p1 = add(p1, r5).astype(BF16)
    grads0, p4 = gate([grads0, p4], [p1, r3])
    r1, r4 = by_xor(p1, "ctx", 1), by_xor(p4, "ctx", 4)
    back0 = exchange(grads0)
    grads1 = attention_bwd(c, 1, cat, probs_t, g_own, g_recv, [p1])
    mixed_own = mix_sum([p0, r1, r3, r4], [grads1])
    (grads1,) = gate([grads1], [back0])
    back1 = exchange(grads1)
    mixed_recv = mirror(mixed_own)
    mixed = mix_out(mixed_own, mixed_recv)
    qkv_grad = jnp.transpose(assemble(back0, back1), (1, 0, 2))

    w_sum = weight_sum(w_own, by_xor(w_other, "dp", 1), [mixed_own])
    w_recv = gate([by_xor(w_sum[x], "dp", 2 * x) for x in range(1, 4)], [mixed_recv])
    w_chip = add(w_sum[0], *w_recv)
    first, second = w_chip[:, :GW], w_chip[:, GW:]
    w_keep = jnp.where(s == 0, first, second)
    w_send = jnp.where(s == 0, second, first).astype(BF16)
    weight_grad = w_keep + other_strand(w_send).astype(F32)
    return (mixed[None, None], qkv_grad[None, None], weight_grad)


def solution(mesh):
    placed = (P("dp", "strand", "ctx", None, None), P("ctx", None), P("dp", "strand", "ctx", None))
    return jax.shard_map(
        body,
        mesh=mesh,
        in_specs=placed,
        out_specs=(
            P("dp", "strand", "ctx", None),
            P("dp", "strand", "ctx", None, None),
            P("ctx", ("dp", "strand")),
        ),
        check_vma=False,
    )
```

```python
import functools
import math

import jax
import jax.numpy as jnp
from jax import lax
from jax.experimental import pallas as pl
from jax.experimental.pallas import tpu as pltpu
from jax.sharding import PartitionSpec as P

DH = 128
N = 8
SEQ = 1024
ROWS = SEQ // N
HALF = ROWS // 2
GW = 256
D = 4096
F32 = jnp.float32
BF16 = jnp.bfloat16
VMEM_LIMIT = 36 * 1024 * 1024


def flip_matrix(n):
    a = lax.broadcasted_iota(jnp.int32, (n, n), 0)
    b = lax.broadcasted_iota(jnp.int32, (n, n), 1)
    return (a + b == n - 1).astype(BF16)


def dot(a, b, ca, cb):
    return lax.dot_general(a, b, (((ca,), (cb,)), ((), ())), preferred_element_type=F32)


def params(limit=VMEM_LIMIT):
    return pltpu.CompilerParams(vmem_limit_bytes=limit)


def cost(flops, nbytes, trans=0):
    return pl.CostEstimate(flops=int(flops), bytes_accessed=int(nbytes), transcendentals=int(trans))


def struct(*shape, dtype=BF16):
    return jax.ShapeDtypeStruct(shape, dtype)


ANY = pl.BlockSpec(memory_space=pl.ANY)


def gate_kernel(*refs):
    pass


def gate(xs, after):
    return pl.pallas_call(
        gate_kernel,
        in_specs=[ANY] * (len(xs) + len(after)),
        out_specs=[ANY] * len(xs),
        out_shape=[struct(*x.shape) for x in xs],
        input_output_aliases={i: i for i in range(len(xs))},
        compiler_params=params(),
        cost_estimate=cost(0, 0),
        name="gate",
    )(*xs, *after)


def gate_kernel(*refs):
    pass


def gate(xs, after):
    return pl.pallas_call(
        gate_kernel,
        in_specs=[ANY] * (len(xs) + len(after)),
        out_specs=[ANY] * len(xs),
        out_shape=[struct(*x.shape) for x in xs],
        input_output_aliases={i: i for i in range(len(xs))},
        compiler_params=params(),
        cost_estimate=cost(0, 0),
        name="gate",
    )(*xs, *after)


def split_kernel(x_ref, out):
    for g in range(N):
        out[g] = x_ref[:, :, GW * g : GW * (g + 1)]


def split(x):
    return pl.pallas_call(
        split_kernel,
        in_specs=[pl.BlockSpec(memory_space=pltpu.VMEM)],
        out_specs=pl.BlockSpec(memory_space=pltpu.VMEM),
        out_shape=struct(N, 3, ROWS, GW),
        compiler_params=params(),
        cost_estimate=cost(0, 2 * 3 * ROWS * 2048 * 2),
        name="split",
    )(x)


def assemble_kernel(blocks, out):
    for g in range(N):
        out[:, :, GW * g : GW * (g + 1)] = blocks[g]


def assemble(blocks):
    return pl.pallas_call(
        assemble_kernel,
        in_specs=[pl.BlockSpec(memory_space=pltpu.VMEM)],
        out_specs=pl.BlockSpec(memory_space=pltpu.VMEM),
        out_shape=struct(3, ROWS, 2048),
        compiler_params=params(),
        cost_estimate=cost(0, 2 * 3 * ROWS * 2048 * 2),
        name="assemble",
    )(blocks)


def upstream_kernel(cot, recv, out):
    flipped = dot(flip_matrix(HALF), recv[...], 1, 0)
    out[...] = (cot[...].astype(F32) + flipped).astype(BF16)


def upstream_rows(cot, recv):
    return pl.pallas_call(
        upstream_kernel,
        grid=(2,),
        in_specs=[pl.BlockSpec((HALF, 2048), lambda k: (0, k))] * 2,
        out_specs=pl.BlockSpec((HALF, 2048), lambda k: (0, k)),
        out_shape=struct(HALF, D),
        compiler_params=params(),
        cost_estimate=cost(2 * 64 * 64 * D, 2 << 20),
        name="upstream_rows",
    )(cot, recv)


def fwd_kernel(c_ref, blocks, *refs):
    cat, att_own, att_send, *probs_t = refs[-5:]
    q = pl.program_id(0)

    @pl.when(q == 0)
    def _():
        flip = flip_matrix(HALF)
        for j in range(N):
            of = jnp.bitwise_xor(c_ref[0], j)
            far = jnp.bitwise_xor(c_ref[0], N - 1 - j)
            cat[1, ROWS * j : ROWS * (j + 1), :] = blocks[of, 1]
            cat[2, ROWS * j : ROWS * (j + 1), :] = blocks[of, 2]
            cat[0, HALF * j : HALF * (j + 1), :] = blocks[of, 0, :HALF, :]
            mirrored = dot(flip, blocks[far, 0, HALF:, :], 1, 0).astype(BF16)
            cat[0, 512 + HALF * j : 512 + HALF * (j + 1), :] = mirrored

    for h in range(2):
        cols = slice(DH * h, DH * (h + 1))
        queries = cat[0, pl.ds(pl.multiple_of(q * 256, 256), 256), cols]
        scores = dot(cat[1, :, cols], queries, 1, 1) * (1.0 / math.sqrt(DH))
        peak = jnp.max(scores, axis=0, keepdims=True)
        expo = jnp.exp(scores - peak)
        probs = (expo * (1.0 / jnp.sum(expo, axis=0, keepdims=True))).astype(BF16)
        probs_t[h][...] = probs
        att = jnp.transpose(dot(cat[2, :, cols], probs, 0, 0)).astype(BF16)

        @pl.when(q < 2)
        def _():
            att_own[:, cols] = att

        @pl.when(q >= 2)
        def _():
            att_send[:, cols] = att


def low_half(q, *_):
    return (jnp.minimum(q, 1), 0)


def high_half(q, *_):
    return (jnp.maximum(q - 2, 0), 0)


def attention_fwd(c, blocks, after):
    return pl.pallas_call(
        fwd_kernel,
        grid_spec=pltpu.PrefetchScalarGridSpec(
            num_scalar_prefetch=1,
            grid=(4,),
            in_specs=[pl.BlockSpec((N, 3, ROWS, GW), lambda q, c_ref: (0, 0, 0, 0))] + [ANY] * len(after),
            out_specs=[
                pl.BlockSpec((3, SEQ, GW), lambda q, c_ref: (0, 0, 0)),
                pl.BlockSpec((256, GW), low_half),
                pl.BlockSpec((256, GW), high_half),
                pl.BlockSpec((SEQ, 256), lambda q, c_ref: (0, q)),
                pl.BlockSpec((SEQ, 256), lambda q, c_ref: (0, q)),
            ],
        ),
        out_shape=[struct(3, SEQ, GW), struct(512, GW), struct(512, GW), struct(SEQ, SEQ), struct(SEQ, SEQ)],
        compiler_params=params(63 * 1024 * 1024),
        cost_estimate=cost(4 * 4 * SEQ * SEQ * DH, 10 << 20, 2 * SEQ * SEQ),
        name="attention_fwd",
    )(c, blocks, *after)


def bwd_kernel(c_ref, cat, probs_t, g_own, g_recv, *refs):
    out, dq, dk, dv = refs[-4:]
    q = pl.program_id(0)
    rows = pl.ds(pl.multiple_of(q * 256, 256), 256)
    queries = cat[0, rows, :]
    grad = jnp.where(q < 2, g_own[...], g_recv[...])
    probs_low = probs_t[...]
    grad_probs = dot(cat[2], grad, 1, 1)
    probs = probs_low.astype(F32)
    product = probs * grad_probs
    centre = jnp.sum(product, axis=0, keepdims=True)
    grad_scores = ((product - probs * centre) * (1.0 / math.sqrt(DH))).astype(BF16)
    part_v = dot(probs_low, grad, 1, 0)
    part_k = dot(grad_scores, queries, 1, 0)

    @pl.when(q == 0)
    def _():
        dv[...] = part_v
        dk[...] = part_k

    @pl.when(q > 0)
    def _():
        dv[...] += part_v
        dk[...] += part_k

    dq[rows, :] = jnp.transpose(dot(cat[1], grad_scores, 0, 0)).astype(BF16)

    @pl.when(q == 3)
    def _():
        flip = flip_matrix(HALF)
        for j in range(N):
            to = jnp.bitwise_xor(c_ref[0], j)
            low = 512 + HALF * (N - 1 - j)
            out[to, 0, :HALF, :] = dq[HALF * j : HALF * (j + 1), :]
            out[to, 0, HALF:, :] = dot(flip, dq[low : low + HALF, :], 1, 0).astype(BF16)
            out[to, 1] = dk[ROWS * j : ROWS * (j + 1), :].astype(BF16)
            out[to, 2] = dv[ROWS * j : ROWS * (j + 1), :].astype(BF16)


def attention_bwd(c, h, cat, probs_t, g_own, g_recv, filled, after):
    return pl.pallas_call(
        bwd_kernel,
        grid_spec=pltpu.PrefetchScalarGridSpec(
            num_scalar_prefetch=1,
            grid=(4,),
            in_specs=[
                pl.BlockSpec((3, SEQ, DH), lambda q, c_ref: (0, 0, h)),
                pl.BlockSpec((SEQ, 256), lambda q, c_ref: (0, q)),
                pl.BlockSpec((256, DH), lambda q, c_ref: (jnp.minimum(q, 1), h)),
                pl.BlockSpec((256, DH), lambda q, c_ref: (jnp.maximum(q - 2, 0), h)),
            ]
            + [ANY] * (len(filled) + len(after)),
            out_specs=pl.BlockSpec((N, 3, ROWS, DH), lambda q, c_ref: (0, 0, 0, h)),
            scratch_shapes=[pltpu.VMEM((SEQ, DH), BF16), pltpu.VMEM((SEQ, DH), F32), pltpu.VMEM((SEQ, DH), F32)],
        ),
        out_shape=struct(N, 3, ROWS, GW),
        input_output_aliases={5 + i: i for i in range(len(filled))},
        compiler_params=params(),
        cost_estimate=cost(4 * 2 * SEQ * SEQ * DH, 4 << 20),
        name="attention_bwd",
    )(c, cat, probs_t, g_own, g_recv, *filled, *after)


def grad_kernel(*refs):
    pieces = refs[:N]
    w = refs[N]
    out, acc = refs[-2:]
    k = pl.program_id(0)
    rows = jnp.concatenate([p[...] for p in pieces], axis=0)
    part = dot(rows, w[...], 1, 1)

    @pl.when(k == 0)
    def _():
        acc[...] = part

    @pl.when(k > 0)
    def _():
        acc[...] += part

    @pl.when(k == 3)
    def _():
        out[...] = acc[...].astype(BF16)


def grad_attended(pieces, w, after):
    return pl.pallas_call(
        grad_kernel,
        grid=(4,),
        in_specs=[pl.BlockSpec((p.shape[0], 1024), lambda k: (0, k)) for p in pieces]
        + [pl.BlockSpec((GW, 1024), lambda k: (0, k))]
        + [ANY] * len(after),
        out_specs=pl.BlockSpec((512, GW), lambda k: (0, 0)),
        out_shape=struct(512, GW),
        scratch_shapes=[pltpu.VMEM((512, GW), F32)],
        compiler_params=params(),
        cost_estimate=cost(2 * 512 * GW * D, 7 << 20),
        name="grad_attended",
    )(*pieces, w, *after)


def project_kernel(own, recv, w, *outs):
    both = (own[...].astype(F32) + recv[...].astype(F32)).astype(BF16)
    part = dot(both, w[...], 1, 0).astype(BF16)
    low = 0
    for out in outs:
        out[...] = part[low : low + out.shape[0], :]
        low += out.shape[0]


def project(own, recv, w):
    rows = (HALF,) * N
    return pl.pallas_call(
        project_kernel,
        grid=(4,),
        in_specs=[
            pl.BlockSpec((512, GW), lambda k: (0, 0)),
            pl.BlockSpec((512, GW), lambda k: (0, 0)),
            pl.BlockSpec((GW, 1024), lambda k: (0, k)),
        ],
        out_specs=[pl.BlockSpec((r, 1024), lambda k: (0, k)) for r in rows],
        out_shape=[struct(r, D) for r in rows],
        compiler_params=params(63 * 1024 * 1024),
        cost_estimate=cost(2 * 512 * GW * D, 7 << 20),
        name="project",
    )(own, recv, w)


def weight_kernel(d_ref, own, recv, *refs):
    pieces = refs[:N]
    out_own, out_other = refs[-2:]
    both = (own[...].astype(F32) + recv[...].astype(F32)).astype(BF16)
    rows = jnp.concatenate([p[...] for p in pieces], axis=0)
    part = dot(both, rows, 0, 0).astype(BF16)
    first, second = part[:, :512], part[:, 512:]
    core = jnp.bitwise_and(d_ref[0], 1)
    out_own[0] = jnp.where(core == 0, first, second)
    out_other[0] = jnp.where(core == 0, second, first)


def weight_part(d, own, recv, pieces, after):
    def columns(x, d_ref):
        return (0, jnp.bitwise_xor(lax.shift_right_logical(d_ref[0], 1), x))

    return pl.pallas_call(
        weight_kernel,
        grid_spec=pltpu.PrefetchScalarGridSpec(
            num_scalar_prefetch=1,
            grid=(4,),
            in_specs=[pl.BlockSpec((512, GW), lambda x, d_ref: (0, 0))] * 2
            + [pl.BlockSpec((p.shape[0], 1024), columns) for p in pieces]
            + [ANY] * len(after),
            out_specs=[pl.BlockSpec((1, GW, 512), lambda x, d_ref: (x, 0, 0))] * 2,
        ),
        out_shape=[struct(4, GW, 512)] * 2,
        compiler_params=params(),
        cost_estimate=cost(2 * 512 * GW * D, 7 << 20),
        name="weight_part",
    )(d, own, recv, *pieces, *after)


def weight_sum_kernel(own, recv, *refs):
    for x in range(4):
        refs[x - 4][...] = add(own[x], recv[x]).astype(BF16)


def weight_sum(own, recv, after):
    return pl.pallas_call(
        weight_sum_kernel,
        in_specs=[pl.BlockSpec(memory_space=pltpu.VMEM)] * 2 + [ANY] * len(after),
        out_specs=[pl.BlockSpec(memory_space=pltpu.VMEM)] * 4,
        out_shape=[struct(GW, 512)] * 4,
        compiler_params=params(),
        cost_estimate=cost(0, 3 << 20),
        name="weight_sum",
    )(own, recv, *after)


def by_xor(x, axis, k):
    return lax.ppermute(x, axis, [(i, i ^ k) for i in range(N)])


def exchange(x):
    return lax.all_to_all(x, "ctx", split_axis=0, concat_axis=0, tiled=True)


def mirror(x):
    return lax.ppermute(x, ("strand", "ctx"), [(i, 2 * N - 1 - i) for i in range(2 * N)])


def other_strand(x):
    return lax.ppermute(x, "strand", [(0, 1), (1, 0)])


def flip_rows(x):
    return dot(flip_matrix(x.shape[0]), x, 1, 0)


def add(*terms):
    total = terms[0].astype(F32)
    for t in terms[1:]:
        total = total + t.astype(F32)
    return total


def mix_sum_kernel(p0, r1, r3, r4, *refs):
    out = refs[-1]
    out[...] = add(p0[...], r1[...], r3[...], r4[...]).astype(BF16)


def mix_sum(terms, after):
    return pl.pallas_call(
        mix_sum_kernel,
        grid=(2,),
        in_specs=[pl.BlockSpec((HALF, 2048), lambda k: (0, k))] * 4 + [ANY] * len(after),
        out_specs=pl.BlockSpec((HALF, 2048), lambda k: (0, k)),
        out_shape=struct(HALF, D),
        compiler_params=params(),
        cost_estimate=cost(0, 5 << 19),
        name="mix_sum",
    )(*terms, *after)


def mix_out_kernel(own, recv, out):
    out[:HALF, :] = own[...]
    out[HALF:, :] = dot(flip_matrix(HALF), recv[...], 1, 0).astype(BF16)


def mix_out(own, recv):
    return pl.pallas_call(
        mix_out_kernel,
        grid=(2,),
        in_specs=[pl.BlockSpec((HALF, 2048), lambda k: (0, k))] * 2,
        out_specs=pl.BlockSpec((ROWS, 2048), lambda k: (0, k)),
        out_shape=struct(ROWS, D),
        compiler_params=params(),
        cost_estimate=cost(0, 2 << 20),
        name="mix_out",
    )(own, recv)


def body(qkv, out_weight, cotangent):
    c = lax.axis_index("ctx").astype(jnp.int32).reshape(1)
    d = lax.axis_index("dp").astype(jnp.int32).reshape(1)
    s = lax.axis_index("strand")
    mine = jnp.transpose(qkv[0, 0], (1, 0, 2))
    cot = cotangent[0, 0]

    cot_recv = mirror(cot[HALF:])
    (sent,) = gate([split(mine)], [cot_recv])
    blocks = exchange(sent)

    u = upstream_rows(cot, cot_recv)
    y1, y3, z = by_xor(u, "ctx", 1), by_xor(u, "ctx", 3), by_xor(u, "ctx", 4)
    y2, zy1, zy3 = by_xor(y3, "ctx", 1), by_xor(y1, "ctx", 4), by_xor(z, "ctx", 3)
    cat, att_own, att_send, *probs_t = attention_fwd(c, blocks, [y1, y3, z])
    att_send, zy3 = gate([att_send, zy3], [y2, zy1])
    att_recv = other_strand(att_send)
    zy2 = by_xor(zy3, "ctx", 1)
    pieces = [u, y1, y2, y3, z, zy1, zy2, zy3]

    p0, p1, p2, p3, p4, p5, p6, p7 = project(att_own, att_recv, out_weight)
    r6, r7, r2 = by_xor(p6, "ctx", 3), by_xor(p7, "ctx", 4), by_xor(p2, "ctx", 1)
    g_own = grad_attended(pieces, out_weight, [p0])
    g_recv = other_strand(g_own)
    p5 = add(p5, r6).astype(BF16)
    r5 = by_xor(p5, "ctx", 4)
    w_own, w_other = weight_part(d, att_own, att_recv, pieces, [g_own, p5])
    p3 = add(p3, r7, r2).astype(BF16)
    r3 = by_xor(p3, "ctx", 3)
    grads = attention_bwd(c, 0, cat, probs_t[0], g_own, g_recv, [], [w_own, p3])
    p1 = add(p1, r5).astype(BF16)
    grads, p4, p1 = gate([grads, p4, p1], [r3])
    r1, r4 = by_xor(p1, "ctx", 1), by_xor(p4, "ctx", 4)
    grads = attention_bwd(c, 1, cat, probs_t[1], g_own, g_recv, [grads], [])
    mixed_own = mix_sum([p0, r1, r3, r4], [grads])
    back = exchange(grads)
    mixed_recv = mirror(mixed_own)
    mixed = mix_out(mixed_own, mixed_recv)
    qkv_grad = jnp.transpose(assemble(back), (1, 0, 2))

    w_sum = weight_sum(w_own, by_xor(w_other, "dp", 1), [mixed_own])
    w_recv = [by_xor(w_sum[x], "dp", 2 * x) for x in range(1, 4)]
    w_recv = gate(w_recv, [mixed_recv])
    w_chip = add(w_sum[0], *w_recv)
    first, second = w_chip[:, :GW], w_chip[:, GW:]
    w_keep = jnp.where(s == 0, first, second)
    w_send = jnp.where(s == 0, second, first).astype(BF16)
    weight_grad = w_keep + other_strand(w_send).astype(F32)
    return (mixed[None, None], qkv_grad[None, None], weight_grad)


def solution(mesh):
    placed = (P("dp", "strand", "ctx", None, None), P("ctx", None), P("dp", "strand", "ctx", None))
    return jax.shard_map(
        body,
        mesh=mesh,
        in_specs=placed,
        out_specs=(
            P("dp", "strand", "ctx", None),
            P("dp", "strand", "ctx", None, None),
            P("ctx", ("dp", "strand")),
        ),
        check_vma=False,
    )
```

```python
import functools
import math

import jax
import jax.numpy as jnp
from jax import lax
from jax.experimental import pallas as pl
from jax.experimental.pallas import tpu as pltpu
from jax.sharding import PartitionSpec as P

DH = 128
N = 8
SEQ = 1024
ROWS = SEQ // N
HALF = ROWS // 2
GW = 256
D = 4096
F32 = jnp.float32
BF16 = jnp.bfloat16
VMEM_LIMIT = 36 * 1024 * 1024


def flip_matrix(n):
    a = lax.broadcasted_iota(jnp.int32, (n, n), 0)
    b = lax.broadcasted_iota(jnp.int32, (n, n), 1)
    return (a + b == n - 1).astype(BF16)


def dot(a, b, ca, cb):
    return lax.dot_general(a, b, (((ca,), (cb,)), ((), ())), preferred_element_type=F32)


def params(limit=VMEM_LIMIT):
    return pltpu.CompilerParams(vmem_limit_bytes=limit)


def cost(flops, nbytes, trans=0):
    return pl.CostEstimate(flops=int(flops), bytes_accessed=int(nbytes), transcendentals=int(trans))


def struct(*shape, dtype=BF16):
    return jax.ShapeDtypeStruct(shape, dtype)


ANY = pl.BlockSpec(memory_space=pl.ANY)


def gate_kernel(*refs):
    pass


def gate(xs, after):
    return pl.pallas_call(
        gate_kernel,
        in_specs=[ANY] * (len(xs) + len(after)),
        out_specs=[ANY] * len(xs),
        out_shape=[struct(*x.shape) for x in xs],
        input_output_aliases={i: i for i in range(len(xs))},
        compiler_params=params(),
        cost_estimate=cost(0, 0),
        name="gate",
    )(*xs, *after)


def gate_kernel(*refs):
    pass


def gate(xs, after):
    return pl.pallas_call(
        gate_kernel,
        in_specs=[ANY] * (len(xs) + len(after)),
        out_specs=[ANY] * len(xs),
        out_shape=[struct(*x.shape) for x in xs],
        input_output_aliases={i: i for i in range(len(xs))},
        compiler_params=params(),
        cost_estimate=cost(0, 0),
        name="gate",
    )(*xs, *after)


def split_kernel(x_ref, out):
    for g in range(N):
        out[g] = x_ref[:, :, GW * g : GW * (g + 1)]


def split(x):
    return pl.pallas_call(
        split_kernel,
        in_specs=[pl.BlockSpec(memory_space=pltpu.VMEM)],
        out_specs=pl.BlockSpec(memory_space=pltpu.VMEM),
        out_shape=struct(N, 3, ROWS, GW),
        compiler_params=params(),
        cost_estimate=cost(0, 2 * 3 * ROWS * 2048 * 2),
        name="split",
    )(x)


def assemble_kernel(blocks, out):
    for g in range(N):
        out[:, :, GW * g : GW * (g + 1)] = blocks[g]


def assemble(blocks):
    return pl.pallas_call(
        assemble_kernel,
        in_specs=[pl.BlockSpec(memory_space=pltpu.VMEM)],
        out_specs=pl.BlockSpec(memory_space=pltpu.VMEM),
        out_shape=struct(3, ROWS, 2048),
        compiler_params=params(),
        cost_estimate=cost(0, 2 * 3 * ROWS * 2048 * 2),
        name="assemble",
    )(blocks)


def upstream_kernel(cot, recv, out):
    flipped = dot(flip_matrix(HALF), recv[...], 1, 0)
    out[...] = (cot[...].astype(F32) + flipped).astype(BF16)


def upstream_rows(cot, recv):
    return pl.pallas_call(
        upstream_kernel,
        grid=(2,),
        in_specs=[pl.BlockSpec((HALF, 2048), lambda k: (0, k))] * 2,
        out_specs=pl.BlockSpec((HALF, 2048), lambda k: (0, k)),
        out_shape=struct(HALF, D),
        compiler_params=params(),
        cost_estimate=cost(2 * 64 * 64 * D, 2 << 20),
        name="upstream_rows",
    )(cot, recv)


def fwd_kernel(c_ref, blocks, *refs):
    cat, att_own, att_send, *probs_t = refs[-5:]
    q = pl.program_id(0)

    @pl.when(q == 0)
    def _():
        flip = flip_matrix(HALF)
        for j in range(N):
            of = jnp.bitwise_xor(c_ref[0], j)
            far = jnp.bitwise_xor(c_ref[0], N - 1 - j)
            cat[1, ROWS * j : ROWS * (j + 1), :] = blocks[of, 1]
            cat[2, ROWS * j : ROWS * (j + 1), :] = blocks[of, 2]
            cat[0, HALF * j : HALF * (j + 1), :] = blocks[of, 0, :HALF, :]
            mirrored = dot(flip, blocks[far, 0, HALF:, :], 1, 0).astype(BF16)
            cat[0, 512 + HALF * j : 512 + HALF * (j + 1), :] = mirrored

    for h in range(2):
        cols = slice(DH * h, DH * (h + 1))
        queries = cat[0, pl.ds(pl.multiple_of(q * 256, 256), 256), cols]
        scores = dot(cat[1, :, cols], queries, 1, 1) * (1.0 / math.sqrt(DH))
        peak = jnp.max(scores, axis=0, keepdims=True)
        expo = jnp.exp(scores - peak)
        probs = (expo * (1.0 / jnp.sum(expo, axis=0, keepdims=True))).astype(BF16)
        probs_t[h][...] = probs
        att = jnp.transpose(dot(cat[2, :, cols], probs, 0, 0)).astype(BF16)

        @pl.when(q < 2)
        def _():
            att_own[:, cols] = att

        @pl.when(q >= 2)
        def _():
            att_send[:, cols] = att


def low_half(q, *_):
    return (jnp.minimum(q, 1), 0)


def high_half(q, *_):
    return (jnp.maximum(q - 2, 0), 0)


def attention_fwd(c, blocks, after):
    return pl.pallas_call(
        fwd_kernel,
        grid_spec=pltpu.PrefetchScalarGridSpec(
            num_scalar_prefetch=1,
            grid=(4,),
            in_specs=[pl.BlockSpec((N, 3, ROWS, GW), lambda q, c_ref: (0, 0, 0, 0))] + [ANY] * len(after),
            out_specs=[
                pl.BlockSpec((3, SEQ, GW), lambda q, c_ref: (0, 0, 0)),
                pl.BlockSpec((256, GW), low_half),
                pl.BlockSpec((256, GW), high_half),
                pl.BlockSpec((SEQ, 256), lambda q, c_ref: (0, q)),
                pl.BlockSpec((SEQ, 256), lambda q, c_ref: (0, q)),
            ],
        ),
        out_shape=[struct(3, SEQ, GW), struct(512, GW), struct(512, GW), struct(SEQ, SEQ), struct(SEQ, SEQ)],
        compiler_params=params(63 * 1024 * 1024),
        cost_estimate=cost(4 * 4 * SEQ * SEQ * DH, 10 << 20, 2 * SEQ * SEQ),
        name="attention_fwd",
    )(c, blocks, *after)


def bwd_kernel(c_ref, cat, probs_t, g_own, g_recv, *refs):
    out, dq, dk, dv = refs[-4:]
    q = pl.program_id(0)
    rows = pl.ds(pl.multiple_of(q * 256, 256), 256)
    queries = cat[0, rows, :]
    grad = jnp.where(q < 2, g_own[...], g_recv[...])
    probs_low = probs_t[...]
    grad_probs = dot(cat[2], grad, 1, 1)
    probs = probs_low.astype(F32)
    product = probs * grad_probs
    centre = jnp.sum(product, axis=0, keepdims=True)
    grad_scores = ((product - probs * centre) * (1.0 / math.sqrt(DH))).astype(BF16)
    part_v = dot(probs_low, grad, 1, 0)
    part_k = dot(grad_scores, queries, 1, 0)

    @pl.when(q == 0)
    def _():
        dv[...] = part_v
        dk[...] = part_k

    @pl.when(q > 0)
    def _():
        dv[...] += part_v
        dk[...] += part_k

    dq[rows, :] = jnp.transpose(dot(cat[1], grad_scores, 0, 0)).astype(BF16)

    @pl.when(q == 3)
    def _():
        flip = flip_matrix(HALF)
        for j in range(N):
            to = jnp.bitwise_xor(c_ref[0], j)
            low = 512 + HALF * (N - 1 - j)
            out[to, 0, :HALF, :] = dq[HALF * j : HALF * (j + 1), :]
            out[to, 0, HALF:, :] = dot(flip, dq[low : low + HALF, :], 1, 0).astype(BF16)
            out[to, 1] = dk[ROWS * j : ROWS * (j + 1), :].astype(BF16)
            out[to, 2] = dv[ROWS * j : ROWS * (j + 1), :].astype(BF16)


def attention_bwd(c, h, cat, probs_t, g_own, g_recv, filled, after):
    return pl.pallas_call(
        bwd_kernel,
        grid_spec=pltpu.PrefetchScalarGridSpec(
            num_scalar_prefetch=1,
            grid=(4,),
            in_specs=[
                pl.BlockSpec((3, SEQ, DH), lambda q, c_ref: (0, 0, h)),
                pl.BlockSpec((SEQ, 256), lambda q, c_ref: (0, q)),
                pl.BlockSpec((256, DH), lambda q, c_ref: (jnp.minimum(q, 1), h)),
                pl.BlockSpec((256, DH), lambda q, c_ref: (jnp.maximum(q - 2, 0), h)),
            ]
            + [ANY] * (len(filled) + len(after)),
            out_specs=pl.BlockSpec((N, 3, ROWS, DH), lambda q, c_ref: (0, 0, 0, h)),
            scratch_shapes=[pltpu.VMEM((SEQ, DH), BF16), pltpu.VMEM((SEQ, DH), F32), pltpu.VMEM((SEQ, DH), F32)],
        ),
        out_shape=struct(N, 3, ROWS, GW),
        input_output_aliases={5 + i: i for i in range(len(filled))},
        compiler_params=params(),
        cost_estimate=cost(4 * 2 * SEQ * SEQ * DH, 4 << 20),
        name="attention_bwd",
    )(c, cat, probs_t, g_own, g_recv, *filled, *after)


def grad_kernel(*refs):
    pieces = refs[:N]
    w = refs[N]
    out, acc = refs[-2:]
    k = pl.program_id(0)
    rows = jnp.concatenate([p[...] for p in pieces], axis=0)
    part = dot(rows, w[...], 1, 1)

    @pl.when(k == 0)
    def _():
        acc[...] = part

    @pl.when(k > 0)
    def _():
        acc[...] += part

    @pl.when(k == 3)
    def _():
        out[...] = acc[...].astype(BF16)


def grad_attended(pieces, w, after):
    return pl.pallas_call(
        grad_kernel,
        grid=(4,),
        in_specs=[pl.BlockSpec((p.shape[0], 1024), lambda k: (0, k)) for p in pieces]
        + [pl.BlockSpec((GW, 1024), lambda k: (0, k))]
        + [ANY] * len(after),
        out_specs=pl.BlockSpec((512, GW), lambda k: (0, 0)),
        out_shape=struct(512, GW),
        scratch_shapes=[pltpu.VMEM((512, GW), F32)],
        compiler_params=params(),
        cost_estimate=cost(2 * 512 * GW * D, 7 << 20),
        name="grad_attended",
    )(*pieces, w, *after)


def project_kernel(own, recv, w, *outs):
    both = (own[...].astype(F32) + recv[...].astype(F32)).astype(BF16)
    part = dot(both, w[...], 1, 0).astype(BF16)
    low = 0
    for out in outs:
        out[...] = part[low : low + out.shape[0], :]
        low += out.shape[0]


def project(own, recv, w):
    rows = (HALF,) * N
    return pl.pallas_call(
        project_kernel,
        grid=(4,),
        in_specs=[
            pl.BlockSpec((512, GW), lambda k: (0, 0)),
            pl.BlockSpec((512, GW), lambda k: (0, 0)),
            pl.BlockSpec((GW, 1024), lambda k: (0, k)),
        ],
        out_specs=[pl.BlockSpec((r, 1024), lambda k: (0, k)) for r in rows],
        out_shape=[struct(r, D) for r in rows],
        compiler_params=params(63 * 1024 * 1024),
        cost_estimate=cost(2 * 512 * GW * D, 7 << 20),
        name="project",
    )(own, recv, w)


def weight_kernel(d_ref, own, recv, *refs):
    pieces = refs[:N]
    out_own, out_other = refs[-2:]
    both = (own[...].astype(F32) + recv[...].astype(F32)).astype(BF16)
    rows = jnp.concatenate([p[...] for p in pieces], axis=0)
    part = dot(both, rows, 0, 0).astype(BF16)
    first, second = part[:, :512], part[:, 512:]
    core = jnp.bitwise_and(d_ref[0], 1)
    out_own[0] = jnp.where(core == 0, first, second)
    out_other[0] = jnp.where(core == 0, second, first)


def weight_part(d, own, recv, pieces, after):
    def columns(x, d_ref):
        return (0, jnp.bitwise_xor(lax.shift_right_logical(d_ref[0], 1), x))

    return pl.pallas_call(
        weight_kernel,
        grid_spec=pltpu.PrefetchScalarGridSpec(
            num_scalar_prefetch=1,
            grid=(4,),
            in_specs=[pl.BlockSpec((512, GW), lambda x, d_ref: (0, 0))] * 2
            + [pl.BlockSpec((p.shape[0], 1024), columns) for p in pieces]
            + [ANY] * len(after),
            out_specs=[pl.BlockSpec((1, GW, 512), lambda x, d_ref: (x, 0, 0))] * 2,
        ),
        out_shape=[struct(4, GW, 512)] * 2,
        compiler_params=params(),
        cost_estimate=cost(2 * 512 * GW * D, 7 << 20),
        name="weight_part",
    )(d, own, recv, *pieces, *after)


def weight_sum_kernel(own, recv, *refs):
    for x in range(4):
        refs[x - 4][...] = add(own[x], recv[x]).astype(BF16)


def weight_sum(own, recv, after):
    return pl.pallas_call(
        weight_sum_kernel,
        in_specs=[pl.BlockSpec(memory_space=pltpu.VMEM)] * 2 + [ANY] * len(after),
        out_specs=[pl.BlockSpec(memory_space=pltpu.VMEM)] * 4,
        out_shape=[struct(GW, 512)] * 4,
        compiler_params=params(),
        cost_estimate=cost(0, 3 << 20),
        name="weight_sum",
    )(own, recv, *after)


def by_xor(x, axis, k):
    return lax.ppermute(x, axis, [(i, i ^ k) for i in range(N)])


def exchange(x):
    return lax.all_to_all(x, "ctx", split_axis=0, concat_axis=0, tiled=True)


def mirror(x):
    return lax.ppermute(x, ("strand", "ctx"), [(i, 2 * N - 1 - i) for i in range(2 * N)])


def other_strand(x):
    return lax.ppermute(x, "strand", [(0, 1), (1, 0)])


def flip_rows(x):
    return dot(flip_matrix(x.shape[0]), x, 1, 0)


def add(*terms):
    total = terms[0].astype(F32)
    for t in terms[1:]:
        total = total + t.astype(F32)
    return total


def mix_sum_kernel(p0, r1, r3, r4, *refs):
    out = refs[-1]
    out[...] = add(p0[...], r1[...], r3[...], r4[...]).astype(BF16)


def mix_sum(terms, after):
    return pl.pallas_call(
        mix_sum_kernel,
        grid=(2,),
        in_specs=[pl.BlockSpec((HALF, 2048), lambda k: (0, k))] * 4 + [ANY] * len(after),
        out_specs=pl.BlockSpec((HALF, 2048), lambda k: (0, k)),
        out_shape=struct(HALF, D),
        compiler_params=params(),
        cost_estimate=cost(0, 5 << 19),
        name="mix_sum",
    )(*terms, *after)


def mix_out_kernel(own, recv, out):
    out[:HALF, :] = own[...]
    out[HALF:, :] = dot(flip_matrix(HALF), recv[...], 1, 0).astype(BF16)


def mix_out(own, recv):
    return pl.pallas_call(
        mix_out_kernel,
        grid=(2,),
        in_specs=[pl.BlockSpec((HALF, 2048), lambda k: (0, k))] * 2,
        out_specs=pl.BlockSpec((ROWS, 2048), lambda k: (0, k)),
        out_shape=struct(ROWS, D),
        compiler_params=params(),
        cost_estimate=cost(0, 2 << 20),
        name="mix_out",
    )(own, recv)


def body(qkv, out_weight, cotangent):
    c = lax.axis_index("ctx").astype(jnp.int32).reshape(1)
    d = lax.axis_index("dp").astype(jnp.int32).reshape(1)
    s = lax.axis_index("strand")
    mine = jnp.transpose(qkv[0, 0], (1, 0, 2))
    cot = cotangent[0, 0]

    cot_recv = mirror(cot[HALF:])
    (sent,) = gate([split(mine)], [cot_recv])
    blocks = exchange(sent)

    u = upstream_rows(cot, cot_recv)
    y1, y3, z = by_xor(u, "ctx", 1), by_xor(u, "ctx", 3), by_xor(u, "ctx", 4)
    y2, zy1, zy3 = by_xor(y3, "ctx", 1), by_xor(y1, "ctx", 4), by_xor(z, "ctx", 3)
    cat, att_own, att_send, *probs_t = attention_fwd(c, blocks, [y1, y3, z])
    att_send, zy3 = gate([att_send, zy3], [y2, zy1])
    att_recv = other_strand(att_send)
    zy2 = by_xor(zy3, "ctx", 1)
    pieces = [u, y1, y2, y3, z, zy1, zy2, zy3]

    p0, p1, p2, p3, p4, p5, p6, p7 = project(att_own, att_recv, out_weight)
    r6, r7, r2 = by_xor(p6, "ctx", 3), by_xor(p7, "ctx", 4), by_xor(p2, "ctx", 1)
    g_own = grad_attended(pieces, out_weight, [p0])
    g_recv = other_strand(g_own)
    p5 = add(p5, r6).astype(BF16)
    r5 = by_xor(p5, "ctx", 4)
    w_own, w_other = weight_part(d, att_own, att_recv, pieces, [g_own, p5])
    p3 = add(p3, r7, r2).astype(BF16)
    r3 = by_xor(p3, "ctx", 3)
    grads = attention_bwd(c, 0, cat, probs_t[0], g_own, g_recv, [], [w_own, p3])
    p1 = add(p1, r5).astype(BF16)
    grads, p4, p1 = gate([grads, p4, p1], [r3])
    r1, r4 = by_xor(p1, "ctx", 1), by_xor(p4, "ctx", 4)
    grads = attention_bwd(c, 1, cat, probs_t[1], g_own, g_recv, [grads], [])
    w_sum = weight_sum(w_own, by_xor(w_other, "dp", 1), [grads])
    mixed_own = mix_sum([p0, r1, r3, r4], [w_sum[0]])
    back = exchange(grads)
    mixed_recv = mirror(mixed_own)
    mixed = mix_out(mixed_own, mixed_recv)
    qkv_grad = jnp.transpose(assemble(back), (1, 0, 2))

    w_recv = [by_xor(w_sum[x], "dp", 2 * x) for x in range(1, 4)]
    w_recv = gate(w_recv, [mixed_recv])
    w_chip = add(w_sum[0], *w_recv)
    first, second = w_chip[:, :GW], w_chip[:, GW:]
    w_keep = jnp.where(s == 0, first, second)
    w_send = jnp.where(s == 0, second, first).astype(BF16)
    weight_grad = w_keep + other_strand(w_send).astype(F32)
    return (mixed[None, None], qkv_grad[None, None], weight_grad)


def solution(mesh):
    placed = (P("dp", "strand", "ctx", None, None), P("ctx", None), P("dp", "strand", "ctx", None))
    return jax.shard_map(
        body,
        mesh=mesh,
        in_specs=placed,
        out_specs=(
            P("dp", "strand", "ctx", None),
            P("dp", "strand", "ctx", None, None),
            P("ctx", ("dp", "strand")),
        ),
        check_vma=False,
    )
```

```python
import functools
import math

import jax
import jax.numpy as jnp
from jax import lax
from jax.experimental import pallas as pl
from jax.experimental.pallas import tpu as pltpu
from jax.sharding import PartitionSpec as P

DH = 128
N = 8
SEQ = 1024
ROWS = SEQ // N
HALF = ROWS // 2
GW = 256
D = 4096
F32 = jnp.float32
BF16 = jnp.bfloat16
VMEM_LIMIT = 36 * 1024 * 1024


def flip_matrix(n):
    a = lax.broadcasted_iota(jnp.int32, (n, n), 0)
    b = lax.broadcasted_iota(jnp.int32, (n, n), 1)
    return (a + b == n - 1).astype(BF16)


def dot(a, b, ca, cb):
    return lax.dot_general(a, b, (((ca,), (cb,)), ((), ())), preferred_element_type=F32)


def params(limit=VMEM_LIMIT):
    return pltpu.CompilerParams(vmem_limit_bytes=limit)


def cost(flops, nbytes, trans=0):
    return pl.CostEstimate(flops=int(flops), bytes_accessed=int(nbytes), transcendentals=int(trans))


def struct(*shape, dtype=BF16):
    return jax.ShapeDtypeStruct(shape, dtype)


ANY = pl.BlockSpec(memory_space=pl.ANY)


def gate_kernel(*refs):
    pass


def gate(xs, after):
    return pl.pallas_call(
        gate_kernel,
        in_specs=[ANY] * (len(xs) + len(after)),
        out_specs=[ANY] * len(xs),
        out_shape=[struct(*x.shape) for x in xs],
        input_output_aliases={i: i for i in range(len(xs))},
        compiler_params=params(),
        cost_estimate=cost(0, 0),
        name="gate",
    )(*xs, *after)


def gate_kernel(*refs):
    pass


def gate(xs, after):
    return pl.pallas_call(
        gate_kernel,
        in_specs=[ANY] * (len(xs) + len(after)),
        out_specs=[ANY] * len(xs),
        out_shape=[struct(*x.shape) for x in xs],
        input_output_aliases={i: i for i in range(len(xs))},
        compiler_params=params(),
        cost_estimate=cost(0, 0),
        name="gate",
    )(*xs, *after)


def split_kernel(x_ref, out):
    for g in range(N):
        out[g] = x_ref[:, :, GW * g : GW * (g + 1)]


def split(x):
    return pl.pallas_call(
        split_kernel,
        in_specs=[pl.BlockSpec(memory_space=pltpu.VMEM)],
        out_specs=pl.BlockSpec(memory_space=pltpu.VMEM),
        out_shape=struct(N, 3, ROWS, GW),
        compiler_params=params(),
        cost_estimate=cost(0, 2 * 3 * ROWS * 2048 * 2),
        name="split",
    )(x)


def assemble_kernel(blocks, out):
    for g in range(N):
        out[:, :, GW * g : GW * (g + 1)] = blocks[g]


def assemble(blocks):
    return pl.pallas_call(
        assemble_kernel,
        in_specs=[pl.BlockSpec(memory_space=pltpu.VMEM)],
        out_specs=pl.BlockSpec(memory_space=pltpu.VMEM),
        out_shape=struct(3, ROWS, 2048),
        compiler_params=params(),
        cost_estimate=cost(0, 2 * 3 * ROWS * 2048 * 2),
        name="assemble",
    )(blocks)


def upstream_kernel(cot, recv, out):
    flipped = dot(flip_matrix(HALF), recv[...], 1, 0)
    out[...] = (cot[...].astype(F32) + flipped).astype(BF16)


def upstream_rows(cot, recv):
    return pl.pallas_call(
        upstream_kernel,
        grid=(2,),
        in_specs=[pl.BlockSpec((HALF, 2048), lambda k: (0, k))] * 2,
        out_specs=pl.BlockSpec((HALF, 2048), lambda k: (0, k)),
        out_shape=struct(HALF, D),
        compiler_params=params(),
        cost_estimate=cost(2 * 64 * 64 * D, 2 << 20),
        name="upstream_rows",
    )(cot, recv)


def fwd_kernel(c_ref, blocks, *refs):
    cat, att_own, att_send, *probs_t = refs[-5:]
    q = pl.program_id(0)

    @pl.when(q == 0)
    def _():
        flip = flip_matrix(HALF)
        for j in range(N):
            of = jnp.bitwise_xor(c_ref[0], j)
            far = jnp.bitwise_xor(c_ref[0], N - 1 - j)
            cat[1, ROWS * j : ROWS * (j + 1), :] = blocks[of, 1]
            cat[2, ROWS * j : ROWS * (j + 1), :] = blocks[of, 2]
            cat[0, HALF * j : HALF * (j + 1), :] = blocks[of, 0, :HALF, :]
            mirrored = dot(flip, blocks[far, 0, HALF:, :], 1, 0).astype(BF16)
            cat[0, 512 + HALF * j : 512 + HALF * (j + 1), :] = mirrored

    for h in range(2):
        cols = slice(DH * h, DH * (h + 1))
        queries = cat[0, pl.ds(pl.multiple_of(q * 256, 256), 256), cols]
        scores = dot(cat[1, :, cols], queries, 1, 1) * (1.0 / math.sqrt(DH))
        peak = jnp.max(scores, axis=0, keepdims=True)
        expo = jnp.exp(scores - peak)
        probs = (expo * (1.0 / jnp.sum(expo, axis=0, keepdims=True))).astype(BF16)
        probs_t[h][...] = probs
        att = jnp.transpose(dot(cat[2, :, cols], probs, 0, 0)).astype(BF16)

        @pl.when(q < 2)
        def _():
            att_own[:, cols] = att

        @pl.when(q >= 2)
        def _():
            att_send[:, cols] = att


def low_half(q, *_):
    return (jnp.minimum(q, 1), 0)


def high_half(q, *_):
    return (jnp.maximum(q - 2, 0), 0)


def attention_fwd(c, blocks, after):
    return pl.pallas_call(
        fwd_kernel,
        grid_spec=pltpu.PrefetchScalarGridSpec(
            num_scalar_prefetch=1,
            grid=(4,),
            in_specs=[pl.BlockSpec((N, 3, ROWS, GW), lambda q, c_ref: (0, 0, 0, 0))] + [ANY] * len(after),
            out_specs=[
                pl.BlockSpec((3, SEQ, GW), lambda q, c_ref: (0, 0, 0)),
                pl.BlockSpec((256, GW), low_half),
                pl.BlockSpec((256, GW), high_half),
                pl.BlockSpec((SEQ, 256), lambda q, c_ref: (0, q)),
                pl.BlockSpec((SEQ, 256), lambda q, c_ref: (0, q)),
            ],
        ),
        out_shape=[struct(3, SEQ, GW), struct(512, GW), struct(512, GW), struct(SEQ, SEQ), struct(SEQ, SEQ)],
        compiler_params=params(63 * 1024 * 1024),
        cost_estimate=cost(4 * 4 * SEQ * SEQ * DH, 10 << 20, 2 * SEQ * SEQ),
        name="attention_fwd",
    )(c, blocks, *after)


def bwd_kernel(c_ref, cat, probs_t, g_own, g_recv, *refs):
    out, dq, dk, dv = refs[-4:]
    q = pl.program_id(0)
    rows = pl.ds(pl.multiple_of(q * 256, 256), 256)
    queries = cat[0, rows, :]
    grad = jnp.where(q < 2, g_own[...], g_recv[...])
    probs_low = probs_t[...]
    grad_probs = dot(cat[2], grad, 1, 1)
    probs = probs_low.astype(F32)
    product = probs * grad_probs
    centre = jnp.sum(product, axis=0, keepdims=True)
    grad_scores = ((product - probs * centre) * (1.0 / math.sqrt(DH))).astype(BF16)
    part_v = dot(probs_low, grad, 1, 0)
    part_k = dot(grad_scores, queries, 1, 0)

    @pl.when(q == 0)
    def _():
        dv[...] = part_v
        dk[...] = part_k

    @pl.when(q > 0)
    def _():
        dv[...] += part_v
        dk[...] += part_k

    dq[rows, :] = jnp.transpose(dot(cat[1], grad_scores, 0, 0)).astype(BF16)

    @pl.when(q == 3)
    def _():
        flip = flip_matrix(HALF)
        for j in range(N):
            to = jnp.bitwise_xor(c_ref[0], j)
            low = 512 + HALF * (N - 1 - j)
            out[to, 0, :HALF, :] = dq[HALF * j : HALF * (j + 1), :]
            out[to, 0, HALF:, :] = dot(flip, dq[low : low + HALF, :], 1, 0).astype(BF16)
            out[to, 1] = dk[ROWS * j : ROWS * (j + 1), :].astype(BF16)
            out[to, 2] = dv[ROWS * j : ROWS * (j + 1), :].astype(BF16)


def attention_bwd(c, h, cat, probs_t, g_own, g_recv, filled, after):
    return pl.pallas_call(
        bwd_kernel,
        grid_spec=pltpu.PrefetchScalarGridSpec(
            num_scalar_prefetch=1,
            grid=(4,),
            in_specs=[
                pl.BlockSpec((3, SEQ, DH), lambda q, c_ref: (0, 0, h)),
                pl.BlockSpec((SEQ, 256), lambda q, c_ref: (0, q)),
                pl.BlockSpec((256, DH), lambda q, c_ref: (jnp.minimum(q, 1), h)),
                pl.BlockSpec((256, DH), lambda q, c_ref: (jnp.maximum(q - 2, 0), h)),
            ]
            + [ANY] * (len(filled) + len(after)),
            out_specs=pl.BlockSpec((N, 3, ROWS, DH), lambda q, c_ref: (0, 0, 0, h)),
            scratch_shapes=[pltpu.VMEM((SEQ, DH), BF16), pltpu.VMEM((SEQ, DH), F32), pltpu.VMEM((SEQ, DH), F32)],
        ),
        out_shape=struct(N, 3, ROWS, GW),
        input_output_aliases={5 + i: i for i in range(len(filled))},
        compiler_params=params(),
        cost_estimate=cost(4 * 2 * SEQ * SEQ * DH, 4 << 20),
        name="attention_bwd",
    )(c, cat, probs_t, g_own, g_recv, *filled, *after)


def grad_kernel(*refs):
    pieces = refs[:N]
    w = refs[N]
    out, acc = refs[-2:]
    k = pl.program_id(0)
    rows = jnp.concatenate([p[...] for p in pieces], axis=0)
    part = dot(rows, w[...], 1, 1)

    @pl.when(k == 0)
    def _():
        acc[...] = part

    @pl.when(k > 0)
    def _():
        acc[...] += part

    @pl.when(k == 1)
    def _():
        out[...] = acc[...].astype(BF16)


def grad_attended(pieces, w, after):
    return pl.pallas_call(
        grad_kernel,
        grid=(2,),
        in_specs=[pl.BlockSpec((p.shape[0], 2048), lambda k: (0, k)) for p in pieces]
        + [pl.BlockSpec((GW, 2048), lambda k: (0, k))]
        + [ANY] * len(after),
        out_specs=pl.BlockSpec((512, GW), lambda k: (0, 0)),
        out_shape=struct(512, GW),
        scratch_shapes=[pltpu.VMEM((512, GW), F32)],
        compiler_params=params(),
        cost_estimate=cost(2 * 512 * GW * D, 7 << 20),
        name="grad_attended",
    )(*pieces, w, *after)


def project_kernel(own, recv, w, *outs):
    both = (own[...].astype(F32) + recv[...].astype(F32)).astype(BF16)
    part = dot(both, w[...], 1, 0).astype(BF16)
    low = 0
    for out in outs:
        out[...] = part[low : low + out.shape[0], :]
        low += out.shape[0]


def project(own, recv, w):
    rows = (HALF,) * N
    return pl.pallas_call(
        project_kernel,
        grid=(2,),
        in_specs=[
            pl.BlockSpec((512, GW), lambda k: (0, 0)),
            pl.BlockSpec((512, GW), lambda k: (0, 0)),
            pl.BlockSpec((GW, 2048), lambda k: (0, k)),
        ],
        out_specs=[pl.BlockSpec((r, 2048), lambda k: (0, k)) for r in rows],
        out_shape=[struct(r, D) for r in rows],
        compiler_params=params(63 * 2048 * 2048),
        cost_estimate=cost(2 * 512 * GW * D, 7 << 20),
        name="project",
    )(own, recv, w)


def weight_kernel(d_ref, own, recv, *refs):
    pieces = refs[:N]
    out_own, out_other = refs[-2:]
    both = (own[...].astype(F32) + recv[...].astype(F32)).astype(BF16)
    rows = jnp.concatenate([p[...] for p in pieces], axis=0)
    part = dot(both, rows, 0, 0).astype(BF16)
    first, second = part[:, :512], part[:, 512:]
    core = jnp.bitwise_and(d_ref[0], 1)
    out_own[0] = jnp.where(core == 0, first, second)
    out_other[0] = jnp.where(core == 0, second, first)


def weight_part(d, own, recv, pieces, after):
    def columns(x, d_ref):
        return (0, jnp.bitwise_xor(lax.shift_right_logical(d_ref[0], 1), x))

    return pl.pallas_call(
        weight_kernel,
        grid_spec=pltpu.PrefetchScalarGridSpec(
            num_scalar_prefetch=1,
            grid=(4,),
            in_specs=[pl.BlockSpec((512, GW), lambda x, d_ref: (0, 0))] * 2
            + [pl.BlockSpec((p.shape[0], 1024), columns) for p in pieces]
            + [ANY] * len(after),
            out_specs=[pl.BlockSpec((1, GW, 512), lambda x, d_ref: (x, 0, 0))] * 2,
        ),
        out_shape=[struct(4, GW, 512)] * 2,
        compiler_params=params(),
        cost_estimate=cost(2 * 512 * GW * D, 7 << 20),
        name="weight_part",
    )(d, own, recv, *pieces, *after)


def weight_sum_kernel(own, recv, *refs):
    for x in range(4):
        refs[x - 4][...] = add(own[x], recv[x]).astype(BF16)


def weight_sum(own, recv, after):
    return pl.pallas_call(
        weight_sum_kernel,
        in_specs=[pl.BlockSpec(memory_space=pltpu.VMEM)] * 2 + [ANY] * len(after),
        out_specs=[pl.BlockSpec(memory_space=pltpu.VMEM)] * 4,
        out_shape=[struct(GW, 512)] * 4,
        compiler_params=params(),
        cost_estimate=cost(0, 3 << 20),
        name="weight_sum",
    )(own, recv, *after)


def by_xor(x, axis, k):
    return lax.ppermute(x, axis, [(i, i ^ k) for i in range(N)])


def exchange(x):
    return lax.all_to_all(x, "ctx", split_axis=0, concat_axis=0, tiled=True)


def mirror(x):
    return lax.ppermute(x, ("strand", "ctx"), [(i, 2 * N - 1 - i) for i in range(2 * N)])


def other_strand(x):
    return lax.ppermute(x, "strand", [(0, 1), (1, 0)])


def flip_rows(x):
    return dot(flip_matrix(x.shape[0]), x, 1, 0)


def add(*terms):
    total = terms[0].astype(F32)
    for t in terms[1:]:
        total = total + t.astype(F32)
    return total


def mix_sum_kernel(p0, r1, r3, r4, *refs):
    out = refs[-1]
    out[...] = add(p0[...], r1[...], r3[...], r4[...]).astype(BF16)


def mix_sum(terms, after):
    return pl.pallas_call(
        mix_sum_kernel,
        grid=(2,),
        in_specs=[pl.BlockSpec((HALF, 2048), lambda k: (0, k))] * 4 + [ANY] * len(after),
        out_specs=pl.BlockSpec((HALF, 2048), lambda k: (0, k)),
        out_shape=struct(HALF, D),
        compiler_params=params(),
        cost_estimate=cost(0, 5 << 19),
        name="mix_sum",
    )(*terms, *after)


def mix_out_kernel(own, recv, out):
    out[:HALF, :] = own[...]
    out[HALF:, :] = dot(flip_matrix(HALF), recv[...], 1, 0).astype(BF16)


def mix_out(own, recv):
    return pl.pallas_call(
        mix_out_kernel,
        grid=(2,),
        in_specs=[pl.BlockSpec((HALF, 2048), lambda k: (0, k))] * 2,
        out_specs=pl.BlockSpec((ROWS, 2048), lambda k: (0, k)),
        out_shape=struct(ROWS, D),
        compiler_params=params(),
        cost_estimate=cost(0, 2 << 20),
        name="mix_out",
    )(own, recv)


def body(qkv, out_weight, cotangent):
    c = lax.axis_index("ctx").astype(jnp.int32).reshape(1)
    d = lax.axis_index("dp").astype(jnp.int32).reshape(1)
    s = lax.axis_index("strand")
    mine = jnp.transpose(qkv[0, 0], (1, 0, 2))
    cot = cotangent[0, 0]

    cot_recv = mirror(cot[HALF:])
    (sent,) = gate([split(mine)], [cot_recv])
    blocks = exchange(sent)

    u = upstream_rows(cot, cot_recv)
    y1, y3, z = by_xor(u, "ctx", 1), by_xor(u, "ctx", 3), by_xor(u, "ctx", 4)
    y2, zy1, zy3 = by_xor(y3, "ctx", 1), by_xor(y1, "ctx", 4), by_xor(z, "ctx", 3)
    cat, att_own, att_send, *probs_t = attention_fwd(c, blocks, [y1, y3, z])
    att_send, zy3 = gate([att_send, zy3], [y2, zy1])
    att_recv = other_strand(att_send)
    zy2 = by_xor(zy3, "ctx", 1)
    pieces = [u, y1, y2, y3, z, zy1, zy2, zy3]

    p0, p1, p2, p3, p4, p5, p6, p7 = project(att_own, att_recv, out_weight)
    r6, r7, r2 = by_xor(p6, "ctx", 3), by_xor(p7, "ctx", 4), by_xor(p2, "ctx", 1)
    g_own = grad_attended(pieces, out_weight, [p0])
    g_recv = other_strand(g_own)
    p5 = add(p5, r6).astype(BF16)
    r5 = by_xor(p5, "ctx", 4)
    w_own, w_other = weight_part(d, att_own, att_recv, pieces, [g_own, p5])
    p3 = add(p3, r7, r2).astype(BF16)
    r3 = by_xor(p3, "ctx", 3)
    grads = attention_bwd(c, 0, cat, probs_t[0], g_own, g_recv, [], [w_own, p3])
    p1 = add(p1, r5).astype(BF16)
    grads, p4, p1 = gate([grads, p4, p1], [r3])
    r1, r4 = by_xor(p1, "ctx", 1), by_xor(p4, "ctx", 4)
    grads = attention_bwd(c, 1, cat, probs_t[1], g_own, g_recv, [grads], [])
    w_sum = weight_sum(w_own, by_xor(w_other, "dp", 1), [grads])
    mixed_own = mix_sum([p0, r1, r3, r4], [w_sum[0]])
    back = exchange(grads)
    mixed_recv = mirror(mixed_own)
    mixed = mix_out(mixed_own, mixed_recv)
    qkv_grad = jnp.transpose(assemble(back), (1, 0, 2))

    w_recv = [by_xor(w_sum[x], "dp", 2 * x) for x in range(1, 4)]
    w_recv = gate(w_recv, [mixed_recv])
    w_chip = add(w_sum[0], *w_recv)
    first, second = w_chip[:, :GW], w_chip[:, GW:]
    w_keep = jnp.where(s == 0, first, second)
    w_send = jnp.where(s == 0, second, first).astype(BF16)
    weight_grad = w_keep + other_strand(w_send).astype(F32)
    return (mixed[None, None], qkv_grad[None, None], weight_grad)


def solution(mesh):
    placed = (P("dp", "strand", "ctx", None, None), P("ctx", None), P("dp", "strand", "ctx", None))
    return jax.shard_map(
        body,
        mesh=mesh,
        in_specs=placed,
        out_specs=(
            P("dp", "strand", "ctx", None),
            P("dp", "strand", "ctx", None, None),
            P("ctx", ("dp", "strand")),
        ),
        check_vma=False,
    )
```
